128 devices in a mesh: fsdp: 32 (over y, x, core), own: 4 (over z).
Axes of the slice: x: 4, y: 4, z: 4, core: 2. Of those that a mesh axis runs over, the one named last changes fastest.
Arguments:
- gradients: bfloat16 [64, 512, 512], P('own', 'fsdp'), may hold values from -120 to 120
- old_stats: float32 [256, 512, 512], P(('fsdp', 'own')), may hold values from -0.25 to 1536, as said below
- stat_slot: int32 [128], replicated, may hold values from 0 to 255, as said below
Outputs:
- update: bfloat16 [64, 512, 512], P('own', 'fsdp')
- new_stats: float32 [256, 512, 512], P(('fsdp', 'own'))
The draws below stay inside these ranges and needn't reach their ends.
Inputs may be any that keep to these rules, and one draw needn't show every extreme that they name: `stat_slot`: statistics 2b and 2b+1 belong to block b, and block b lies on own index b // 16. Every statistic has a slot of its own; slot g lies on device g // 2, devices numbered with fsdp slowest. The statistics of the blocks of own index j lie in slots of devices with own index (j + 2) mod 4. Some device holds 2 statistics. `old_stats`: every slot is symmetric, and each diagonal entry exceeds the sum of the magnitudes of the other entries of its row.
All inputs are finite; a program needn't handle non-finite values.
Results may differ from the reference program's by a relative error of at most 0.0071.
Values may be sent and summed in bfloat16 or wider, within the bound.
A program may use at most 128 MiB of HBM per device.

```python
import jax
import jax.numpy as jnp
from jax import lax

B = 512
ITERS = 6
CAP = 2
NBLK = 64
NSTAT = 128
SLOTS = 256
N_FSDP = 32
N_OWN = 4


def draw_gradients(key, part):
    key = jax.random.fold_in(key, 5)
    first, second, third = jax.random.split(key, 3)
    position = jnp.arange(B, dtype=jnp.float32) / B
    trend = (3.0 ** (position - 0.5))[None, :, None]
    row_rough = 10.0 ** (jax.random.uniform(second, (NBLK, B, 1), jnp.float32) - 0.5)
    col_rough = 10.0 ** (jax.random.uniform(third, (NBLK, 1, B), jnp.float32) - 0.5)
    base = jnp.clip(jax.random.normal(first, (NBLK, B, B), jnp.float32), -4.0, 4.0)
    return (base * trend * row_rough * col_rough).astype(jnp.bfloat16)


def draw_old_stats(key, part):
    key = jax.random.fold_in(key, 7)
    first, second = jax.random.split(key, 2)
    raw = jax.random.uniform(first, (SLOTS, B, B), jnp.float32, -0.25, 0.25)
    symmetric = 0.5 * (raw + jnp.swapaxes(raw, 1, 2))
    spread = 10.0 ** jax.random.uniform(second, (SLOTS, B), jnp.float32, -0.3, 0.9)
    diagonal = 0.25 * B * (1.0 + spread)
    rows = jnp.arange(B)
    on_diagonal = rows[:, None] == rows[None, :]
    return jnp.where(on_diagonal[None], diagonal[:, :, None], symmetric)


def column_slots(subkey):
    first, second, third, fourth = jax.random.split(subkey, 4)
    per_column = NSTAT // N_OWN
    doubles = jax.random.randint(first, (), 1, N_FSDP // 2 + 1)
    row_order = jax.random.permutation(second, N_FSDP)
    position = jnp.arange(per_column)
    is_double = position < 2 * doubles
    later = jnp.clip(position - doubles, 0, N_FSDP - 1)
    row_pick = jnp.where(is_double, row_order[jnp.clip(position // 2, 0, N_FSDP - 1)], row_order[later])
    single_slot = jax.random.randint(third, (per_column,), 0, 2)
    cap_pick = jnp.where(is_double, position % 2, single_slot)
    order = jax.random.permutation(fourth, per_column)
    return (row_pick[order], cap_pick[order])


def draw_stat_slot(key, part):
    key = jax.random.fold_in(key, 11)
    rows, caps = jax.vmap(column_slots)(jax.random.split(key, N_OWN))
    columns = jnp.arange(N_OWN)
    owner_col = ((columns + N_OWN // 2) % N_OWN)[:, None]
    slot_index = (rows * N_OWN + owner_col) * CAP + caps
    return slot_index.reshape(NSTAT).astype(jnp.int32)


def setup_inputs(seed: int = 0) -> dict:
    seeds = jax.random.split(jax.random.key(seed), 4)
    gradients = draw_gradients(jax.random.fold_in(seeds[3], 71), 0)
    old_stats = draw_old_stats(jax.random.fold_in(seeds[3], 71), 0)
    stat_slot = draw_stat_slot(jax.random.fold_in(seeds[3], 71), 0)
    return {"gradients": gradients, "old_stats": old_stats, "stat_slot": stat_slot}


keep_weight = 0.9
fresh_weight = 0.1
graft_eps = 1e-06

def product(left_side, right_side):
    return jnp.matmul(left_side, right_side, precision=lax.Precision.HIGHEST)

def inverse_root(matrix):
    identity = jnp.eye(B, dtype=jnp.float32)
    trace_value = jnp.trace(matrix)
    moment = matrix / trace_value
    inverse = identity * trace_value ** (-0.25)
    for sweep in range(ITERS):
        factor = (5.0 * identity - moment) * 0.25
        inverse = product(inverse, factor)
        square = product(factor, factor)
        moment = product(square, product(square, moment))
    return inverse

def reference(gradients, old_stats, stat_slot):

    def one_stat(stat_index):
        grad_block = gradients[stat_index // 2]
        oriented = jnp.where(stat_index % 2 == 1, grad_block.T, grad_block)
        gram_matrix = jnp.dot(oriented, oriented.T, preferred_element_type=jnp.float32)
        updated = keep_weight * old_stats[stat_slot[stat_index]] + fresh_weight * gram_matrix
        return (updated, inverse_root(updated).astype(jnp.bfloat16))
    updated_all, roots = lax.map(one_stat, jnp.arange(NSTAT, dtype=jnp.int32))
    new_stats = old_stats.at[stat_slot].set(updated_all)

    def one_block(operands):
        grad_block, left_root, right_root = operands
        hidden = jnp.dot(left_root, grad_block, preferred_element_type=jnp.float32).astype(jnp.bfloat16)
        shaped = jnp.dot(hidden, right_root, preferred_element_type=jnp.float32)
        grad_wide = grad_block.astype(jnp.float32)
        grad_norm = jnp.sum(grad_wide * grad_wide)
        shaped_norm = jnp.sum(shaped * shaped)
        return (shaped * jnp.sqrt(grad_norm / (shaped_norm + graft_eps))).astype(jnp.bfloat16)
    update = lax.map(one_block, (gradients, roots[0::2], roots[1::2]))
    return (update, new_stats)
```

```python
import functools

import jax
import jax.numpy as jnp
from jax import lax
from jax.experimental import pallas as pl
from jax.experimental.pallas import tpu as pltpu
from jax.sharding import PartitionSpec as P

ITERS = 6
CAPS = 2

keep_weight = 0.9
fresh_weight = 0.1
graft_eps = 1e-06

MESH = pl.DeviceIdType.MESH
BF16 = jnp.bfloat16
F32 = jnp.float32


def product(left_side, right_side):
    return jnp.dot(left_side, right_side, preferred_element_type=F32)


def rows_gram(block):
    return lax.dot_general(block, block, (((1,), (1,)), ((), ())), preferred_element_type=F32)


def columns_gram(block):
    return lax.dot_general(block, block, (((0,), (0,)), ((), ())), preferred_element_type=F32)


def total(values):
    return jnp.sum(jnp.sum(values, axis=0, keepdims=True), axis=1, keepdims=True)


def diagonal_mask(width):
    rows = lax.broadcasted_iota(jnp.int32, (width, width), 0)
    return rows == lax.broadcasted_iota(jnp.int32, (width, width), 1)


def kernel(
    slot_ref, table_ref, grad_ref, old_ref,
    update_ref, new_ref,
    old_wide, spread, gathered, chosen, old_rows, far_rows, block_rows,
    routed, routed_in, roots, moment, moment_low, gap_low, mixed_low, inverse, out_rows,
    load_sem, local_sem, send_sems, recv_sems,
):
    fsdp_count = spread.shape[0]
    own_count = lax.axis_size("own")
    chip_count = fsdp_count // 2
    row_count, width = grad_ref.shape[1:]
    f = lax.axis_index("fsdp")
    q = lax.axis_index("own")
    far = lax.rem(q + own_count // 2, own_count)
    core = lax.rem(f, 2)
    chip = f // 2
    sibling = f + 1 - 2 * core

    def peer(d):
        return lax.rem(f + d, fsdp_count)

    def push(src, dst, phase, row, plane):
        return pltpu.make_async_remote_copy(
            src_ref=src,
            dst_ref=dst,
            send_sem=send_sems.at[phase],
            recv_sem=recv_sems.at[phase],
            device_id={"fsdp": row, "own": plane},
            device_id_type=MESH,
        )

    def arrived(ref, phase):
        pltpu.make_async_copy(ref, ref, recv_sems.at[phase]).wait()

    def left_here(ref, phase):
        pltpu.make_async_copy(ref, ref, send_sems.at[phase]).wait()

    loads = [
        pltpu.make_async_copy(old_ref.at[c], old_wide.at[c], load_sem.at[c]) for c in range(CAPS)
    ]
    for load in loads:
        load.start()

    barrier = pltpu.get_barrier_semaphore()

    @pl.loop(1, fsdp_count)
    def _(d):
        pl.semaphore_signal(
            barrier, inc=1, device_id={"fsdp": peer(d), "own": q}, device_id_type=MESH
        )

    @pl.loop(0, fsdp_count)
    def _(d):
        pl.semaphore_signal(
            barrier, inc=1, device_id={"fsdp": peer(d), "own": far}, device_id_type=MESH
        )

    for c in range(CAPS):
        loads[c].wait()

        @pl.loop(0, fsdp_count)
        def _(r):
            rows = pl.ds(pl.multiple_of(r * row_count, row_count), row_count)
            spread[r, c] = old_wide[c, rows, :].astype(BF16)

    pl.semaphore_wait(barrier, 2 * fsdp_count - 1)

    @pl.loop(1, fsdp_count)
    def _(d):
        t = peer(d)
        push(spread.at[t], gathered.at[f], 0, t, q).start()

    own_spread = pltpu.make_async_copy(spread.at[f], gathered.at[f], recv_sems.at[0])
    own_spread.start()

    far_push = push(grad_ref, far_rows, 1, f, far)
    far_push.start()

    @pl.loop(1, chip_count)
    def _(d):
        t = lax.rem(chip + d, chip_count)
        push(grad_ref.at[t], block_rows.at[chip, core], 2, 2 * t + core, q).start()

    pltpu.make_async_copy(grad_ref.at[chip], block_rows.at[chip, core], recv_sems.at[2]).start()
    arrived(block_rows.at[:, core], 2)
    swap = push(block_rows.at[:, core], block_rows.at[:, core], 3, sibling, q)
    swap.start()

    arrived(gathered, 0)

    @pl.loop(0, fsdp_count)
    def _(d):
        t = peer(d)
        slot = slot_ref[far * fsdp_count + t]
        chosen[t] = gathered[slot // (CAPS * own_count), lax.rem(slot, CAPS)]
        push(chosen.at[t], old_rows.at[f], 4, t, far).start()

    far_push.wait_recv()

    def choose(t):
        for c in range(CAPS):
            entry = table_ref[t * CAPS + c]
            routed[t, c] = far_rows[lax.max(entry - 1, 0) // 2]

    @pl.loop(1, fsdp_count)
    def _(d):
        t = peer(d)
        choose(t)
        push(routed.at[t], routed_in.at[f], 5, t, q).start()

    choose(f)
    pltpu.make_async_copy(routed.at[f], routed_in.at[f], recv_sems.at[5]).start()

    swap.wait()
    block = block_rows[...].reshape(width, width)
    wide = block.astype(F32)
    grad_total = total(wide * wide)

    @pl.when(core == 0)
    def _():
        moment[...] = rows_gram(block)

    @pl.when(core == 1)
    def _():
        moment[...] = columns_gram(block)

    arrived(old_rows, 4)
    on_diagonal = diagonal_mask(width)
    statistic = keep_weight * old_rows[...].reshape(width, width).astype(F32) + (
        fresh_weight * moment[...]
    )
    trace_value = total(jnp.where(on_diagonal, statistic, 0.0))
    start = statistic * (1.0 / trace_value)
    moment[...] = start
    moment_low[...] = start.astype(BF16)
    inverse[...] = -0.25 * start

    def sweep(step, level):
        low = moment_low[...]
        gap_low[...] = (product(low, low) - 10.0 * moment[...]).astype(BF16)
        mixed = (25.0 * moment[...] + product(gap_low[...], low)) * (1.0 / 16.0)
        mixed_low[...] = mixed.astype(BF16)
        fresh = (25.0 * mixed + product(gap_low[...], mixed_low[...])) * (1.0 / 16.0)
        moment[...] = fresh
        moment_low[...] = fresh.astype(BF16)
        inverse[...] = 1.25 * inverse[...] - 0.25 * (
            level * fresh + product(inverse[...].astype(BF16), moment_low[...])
        )
        return level * 1.25

    level = lax.fori_loop(0, ITERS - 1, sweep, jnp.float32(1.25))
    scale = 1.0 / jnp.sqrt(jnp.sqrt(trace_value))
    root = (jnp.where(on_diagonal, level, 0.0) + inverse[...]) * scale
    roots[core] = root.astype(BF16)
    trade = push(roots.at[core], roots.at[core], 6, sibling, q)
    trade.start()
    trade.wait()

    hidden = product(roots[0], block).astype(BF16)
    shaped = product(hidden, roots[1])
    ratio = jnp.sqrt(grad_total / (total(shaped * shaped) + graft_eps))
    out_rows[...] = (shaped * ratio).astype(BF16).reshape(out_rows.shape)

    @pl.loop(1, chip_count)
    def _(d):
        t = lax.rem(chip + d, chip_count)
        push(out_rows.at[t, core], update_ref.at[chip], 7, 2 * t + core, q).start()

    pltpu.make_async_copy(out_rows.at[chip, core], update_ref.at[chip], recv_sems.at[7]).start()

    arrived(routed_in, 5)
    for c in range(CAPS):
        entry = table_ref[f * CAPS + c]
        used = entry > 0
        odd = lax.rem(lax.max(entry - 1, 0), 2) == 1
        keep = jnp.where(used, keep_weight, 1.0)
        fresh = jnp.where(used, fresh_weight, 0.0)
        fresh_right = jnp.where(odd, fresh, 0.0)
        source = routed_in[:, c].reshape(width, width)
        gram = (fresh - fresh_right) * rows_gram(source) + fresh_right * columns_gram(source)
        old_wide[c] = keep * old_wide[c] + gram
        pltpu.make_async_copy(old_wide.at[c], new_ref.at[c], load_sem.at[c]).start()

    for c in range(CAPS):
        pltpu.make_async_copy(old_wide.at[c], new_ref.at[c], load_sem.at[c]).wait()
    arrived(update_ref, 7)

    left_here(spread.at[pl.ds(0, fsdp_count - 1)], 0)
    far_push.wait_send()
    left_here(grad_ref.at[pl.ds(0, chip_count - 1)], 2)
    left_here(chosen, 4)
    left_here(routed.at[pl.ds(0, fsdp_count - 1)], 5)
    left_here(out_rows.at[pl.ds(0, chip_count - 1), 0], 7)


def body(gradients, old_stats, stat_slot):
    fsdp_count = lax.axis_size("fsdp")
    own_count = lax.axis_size("own")
    blk_count, row_count, width = gradients.shape
    far = (lax.axis_index("own") + own_count // 2) % own_count
    slots = lax.dynamic_slice_in_dim(stat_slot, far * fsdp_count, fsdp_count)
    places = slots // (CAPS * own_count) * CAPS + slots % CAPS
    place_ids = jnp.arange(fsdp_count * CAPS, dtype=jnp.int32)
    stat_ids = jnp.arange(1, fsdp_count + 1, dtype=jnp.int32)
    table = jnp.sum(
        jnp.where(places[None, :] == place_ids[:, None], stat_ids[None, :], 0), axis=1
    ).astype(jnp.int32)

    square = (width, width)
    vmem = pltpu.VMEM
    return pl.pallas_call(
        kernel,
        out_shape=(
            jax.ShapeDtypeStruct(gradients.shape, gradients.dtype),
            jax.ShapeDtypeStruct(old_stats.shape, old_stats.dtype),
        ),
        in_specs=[
            pl.BlockSpec(memory_space=pltpu.SMEM),
            pl.BlockSpec(memory_space=pltpu.SMEM),
            pl.BlockSpec(memory_space=pl.ANY),
            pl.BlockSpec(memory_space=pl.ANY),
        ],
        out_specs=(pl.BlockSpec(memory_space=pl.ANY), pl.BlockSpec(memory_space=pl.ANY)),
        scratch_shapes=[
            vmem((CAPS, *square), F32),
            vmem((fsdp_count, CAPS, row_count, width), BF16),
            vmem((fsdp_count, CAPS, row_count, width), BF16),
            vmem((fsdp_count, row_count, width), BF16),
            vmem((fsdp_count, row_count, width), BF16),
            vmem((blk_count, row_count, width), BF16),
            vmem((fsdp_count // 2, 2, row_count, width), BF16),
            vmem((fsdp_count, CAPS, row_count, width), BF16),
            vmem((fsdp_count, CAPS, row_count, width), BF16),
            vmem((2, *square), BF16),
            vmem(square, F32),
            vmem(square, BF16),
            vmem(square, BF16),
            vmem(square, BF16),
            vmem(square, F32),
            vmem((fsdp_count // 2, 2, row_count, width), BF16),
            pltpu.SemaphoreType.DMA((CAPS,)),
            pltpu.SemaphoreType.DMA((1,)),
            pltpu.SemaphoreType.DMA((8,)),
            pltpu.SemaphoreType.DMA((8,)),
        ],
        compiler_params=pltpu.CompilerParams(
            collective_id=0, has_side_effects=True, vmem_limit_bytes=48 * 2**20
        ),
        cost_estimate=pl.CostEstimate(
            flops=60 * width**3, bytes_accessed=5 * 2**20, transcendentals=0
        ),
    )(stat_slot, table, gradients, old_stats)


def solution(mesh):
    return jax.shard_map(
        body,
        mesh=mesh,
        in_specs=(P("own", "fsdp", None), P(("fsdp", "own"), None, None), P()),
        out_specs=(P("own", "fsdp", None), P(("fsdp", "own"), None, None)),
        check_vma=False,
    )
```

```python
import math

import jax
import jax.numpy as jnp
from jax import lax
from jax.experimental import pallas as pl
from jax.experimental.pallas import tpu as pltpu
from jax.sharding import PartitionSpec as P

ITERS = 6
CAPS = 2
SPLIT = 4

keep_weight = 0.9
fresh_weight = 0.1
graft_eps = 1e-06

MESH = pl.DeviceIdType.MESH
BF16 = jnp.bfloat16
F32 = jnp.float32


def product(left_side, right_side):
    return jnp.dot(left_side, right_side, preferred_element_type=F32)


def rows_gram(block):
    return lax.dot_general(block, block, (((1,), (1,)), ((), ())), preferred_element_type=F32)


def columns_gram(block):
    return lax.dot_general(block, block, (((0,), (0,)), ((), ())), preferred_element_type=F32)


def total(values):
    return jnp.sum(jnp.sum(values, axis=0, keepdims=True), axis=1, keepdims=True)


def diagonal_mask(width):
    rows = lax.broadcasted_iota(jnp.int32, (width, width), 0)
    return rows == lax.broadcasted_iota(jnp.int32, (width, width), 1)


def upper_blocks(width):
    side = width // SPLIT
    pairs = [(i, j) for i in range(SPLIT) for j in range(i, SPLIT)]
    return side, [(pl.ds(i * side, side), pl.ds(j * side, side)) for i, j in pairs]


def kernel(
    slot_ref, grad_ref, old_ref,
    update_ref, new_ref,
    slots, slot_row, table_row, table,
    old_wide, spread_a, spread_b, gathered_a, gathered_b, chosen_a, chosen_b, old_rows,
    far_rows, block_rows, routed, routed_in, roots,
    moment, moment_low, gap_low, mixed_low, inverse, out_rows,
    load_sem, small_sem, send_sems, recv_sems,
):
    chip_count = spread_a.shape[0]
    fsdp_count = 2 * chip_count
    chip_side = math.isqrt(chip_count)
    own_count = lax.axis_size("own")
    row_count, width = grad_ref.shape[1:]
    stat_count = slot_ref.shape[1]
    f = lax.axis_index("fsdp")
    q = lax.axis_index("own")
    far = lax.rem(q + own_count // 2, own_count)
    core = lax.rem(f, 2)
    chip = f // 2
    sibling = f + 1 - 2 * core
    parts_a = spread_a.shape[2]
    parts_b = spread_b.shape[2]

    def chip_at(d):
        turn = lax.rem(5 * d, chip_count)
        y = lax.rem(chip // chip_side + turn // chip_side, chip_side)
        x = lax.rem(chip + turn, chip_side)
        return y * chip_side + x

    def push(src, dst, phase, row, plane):
        return pltpu.make_async_remote_copy(
            src_ref=src,
            dst_ref=dst,
            send_sem=send_sems.at[phase],
            recv_sem=recv_sems.at[phase],
            device_id={"fsdp": row, "own": plane},
            device_id_type=MESH,
        )

    def keep_here(src, dst, phase):
        pltpu.make_async_copy(src, dst, recv_sems.at[phase]).start()

    def arrived(ref, phase):
        pltpu.make_async_copy(ref, ref, recv_sems.at[phase]).wait()

    def left_here(ref, phase):
        pltpu.make_async_copy(ref, ref, send_sems.at[phase]).wait()

    loads = [
        pltpu.make_async_copy(old_ref.at[c], old_wide.at[c], load_sem.at[c]) for c in range(CAPS)
    ]
    slot_loads = [
        pltpu.make_async_copy(slot_ref, slots, small_sem.at[0]),
        pltpu.make_async_copy(slot_ref, slot_row, small_sem.at[1]),
    ]
    for load in loads + slot_loads:
        load.start()

    barrier = pltpu.get_barrier_semaphore()

    def greet(row, plane):
        pl.semaphore_signal(
            barrier, inc=1, device_id={"fsdp": row, "own": plane}, device_id_type=MESH
        )

    @pl.loop(1, fsdp_count)
    def _(d):
        greet(lax.rem(f + d, fsdp_count), q)

    greet(f, far)

    side, uppers = upper_blocks(width)
    pieces = side // row_count
    for c in range(CAPS):
        loads[c].wait()
        for b, (rows, columns) in enumerate(uppers):
            low = old_wide[c, rows, columns].astype(BF16).reshape(pieces, row_count, side)
            for piece in range(pieces):
                target, part = divmod(b * pieces + piece, parts_a + parts_b)
                if part < parts_a:
                    spread_a[target, c, part] = low[piece]
                else:
                    spread_b[target, c, part - parts_a] = low[piece]

    pl.semaphore_wait(barrier, fsdp_count)

    far_push = push(grad_ref, far_rows, 1, f, far)
    far_push.start()

    def spread_to(source, target, e):
        @pl.loop(1, chip_count)
        def _(d):
            t = chip_at(d)
            push(source.at[t], target.at[f], 0, 2 * t + e, q).start()

    @pl.when(core == 0)
    def _():
        spread_to(spread_a, gathered_a, 0)
        spread_to(spread_b, gathered_b, 1)
        push(spread_b.at[chip], gathered_b.at[f], 0, sibling, q).start()
        keep_here(spread_a.at[chip], gathered_a.at[f], 0)

    @pl.when(core == 1)
    def _():
        spread_to(spread_b, gathered_b, 1)
        spread_to(spread_a, gathered_a, 0)
        push(spread_a.at[chip], gathered_a.at[f], 0, sibling, q).start()
        keep_here(spread_b.at[chip], gathered_b.at[f], 0)

    @pl.loop(1, chip_count)
    def _(d):
        t = chip_at(d)
        push(grad_ref.at[t], block_rows.at[chip, core], 2, 2 * t + core, q).start()

    keep_here(grad_ref.at[chip], block_rows.at[chip, core], 2)

    for load in slot_loads:
        load.wait()
    grid = (stat_count, stat_count)
    by_stat = jnp.transpose(jnp.broadcast_to(slot_row[...], grid))
    place = jnp.right_shift(by_stat, 3) * CAPS + jnp.bitwise_and(by_stat, 1)
    here = jnp.bitwise_and(jnp.right_shift(by_stat, 1), 3) == q
    hit = here & (place == lax.broadcasted_iota(jnp.int32, grid, 1))
    names = lax.broadcasted_iota(jnp.int32, grid, 0) + 1
    table_row[...] = jnp.sum(jnp.where(hit, names, 0), axis=0, keepdims=True)
    table_copy = pltpu.make_async_copy(table_row, table, small_sem.at[0])
    table_copy.start()
    table_copy.wait()

    arrived(block_rows.at[:, core], 2)
    swap = push(block_rows.at[:, core], block_rows.at[:, core], 3, sibling, q)
    swap.start()

    far_push.wait_recv()

    @pl.loop(0, fsdp_count)
    def _(t):
        for c in range(CAPS):
            entry = lax.max(table[0, t * CAPS + c] - 1, 0)
            routed[t, c] = far_rows[lax.rem(entry, fsdp_count) // 2]

    def forward(gathered, chosen, first, parts):
        arrived(gathered, 0)

        @pl.loop(0, chip_count)
        def _(d):
            for e in range(2):
                t = 2 * chip_at(d) + e
                slot = slots[0, far * fsdp_count + t]
                chosen[t] = gathered[slot // (CAPS * own_count), lax.rem(slot, CAPS)]
                push(chosen.at[t], old_rows.at[chip, pl.ds(first, parts)], 4, t, far).start()

    @pl.when(core == 0)
    def _():
        forward(gathered_a, chosen_a, 0, parts_a)

    @pl.when(core == 1)
    def _():
        forward(gathered_b, chosen_b, parts_a, parts_b)

    @pl.loop(1, chip_count)
    def _(d):
        for e in range(2):
            t = 2 * chip_at(d) + e
            push(routed.at[t], routed_in.at[f], 5, t, q).start()

    push(routed.at[sibling], routed_in.at[f], 5, sibling, q).start()
    keep_here(routed.at[f], routed_in.at[f], 5)

    swap.wait()
    block = block_rows[...].reshape(width, width)
    wide = block.astype(F32)
    grad_total = total(wide * wide)

    @pl.when(core == 0)
    def _():
        moment[...] = rows_gram(block)

    @pl.when(core == 1)
    def _():
        moment[...] = columns_gram(block)

    arrived(old_rows, 4)
    on_diagonal = diagonal_mask(side)
    upper = old_rows[...].reshape(len(uppers), side, side)
    trace_value = jnp.zeros((1, 1), F32)
    for b, (rows, columns) in enumerate(uppers):
        old = keep_weight * upper[b].astype(F32)
        fresh = old + fresh_weight * moment[rows, columns]
        moment[rows, columns] = fresh
        if rows == columns:
            trace_value += total(jnp.where(on_diagonal, fresh, 0.0))
        else:
            moment[columns, rows] = jnp.transpose(fresh)
    start = moment[...] * (1.0 / trace_value)
    moment[...] = start
    moment_low[...] = start.astype(BF16)
    inverse[...] = -0.25 * start

    def sweep(step, level):
        low = moment_low[...]
        gap_low[...] = (product(low, low) - 10.0 * moment[...]).astype(BF16)
        mixed = (25.0 * moment[...] + product(gap_low[...], low)) * (1.0 / 16.0)
        mixed_low[...] = mixed.astype(BF16)
        fresh = (25.0 * mixed + product(gap_low[...], mixed_low[...])) * (1.0 / 16.0)
        moment[...] = fresh
        moment_low[...] = fresh.astype(BF16)
        inverse[...] = 1.25 * inverse[...] - 0.25 * (
            level * fresh + product(inverse[...].astype(BF16), moment_low[...])
        )
        return level * 1.25

    level = lax.fori_loop(0, ITERS - 1, sweep, jnp.float32(1.25))
    scale = 1.0 / jnp.sqrt(jnp.sqrt(trace_value))
    root = (jnp.where(diagonal_mask(width), level, 0.0) + inverse[...]) * scale
    roots[core] = root.astype(BF16)
    trade = push(roots.at[core], roots.at[core], 6, sibling, q)
    trade.start()
    trade.wait()

    hidden = product(roots[0], block).astype(BF16)
    shaped = product(hidden, roots[1])
    ratio = jnp.sqrt(grad_total / (total(shaped * shaped) + graft_eps))
    out_rows[...] = (shaped * ratio).astype(BF16).reshape(out_rows.shape)

    @pl.loop(1, chip_count)
    def _(d):
        t = chip_at(d)
        push(out_rows.at[t, core], update_ref.at[chip], 7, 2 * t + core, q).start()

    keep_here(out_rows.at[chip, core], update_ref.at[chip], 7)

    arrived(routed_in, 5)
    for c in range(CAPS):
        entry = table[0, f * CAPS + c]
        used = entry > 0
        odd = lax.rem(lax.max(entry - 1, 0), 2) == 1
        keep = jnp.where(used, keep_weight, 1.0)
        fresh = jnp.where(used, fresh_weight, 0.0)
        fresh_right = jnp.where(odd, fresh, 0.0)
        source = routed_in[:, c].reshape(width, width)
        gram = (fresh - fresh_right) * rows_gram(source) + fresh_right * columns_gram(source)
        old_wide[c] = keep * old_wide[c] + gram
        pltpu.make_async_copy(old_wide.at[c], new_ref.at[c], load_sem.at[c]).start()

    for c in range(CAPS):
        pltpu.make_async_copy(old_wide.at[c], new_ref.at[c], load_sem.at[c]).wait()
    arrived(update_ref, 7)

    @pl.when(core == 0)
    def _():
        left_here(spread_a.at[pl.ds(0, chip_count - 1)], 0)
        left_here(spread_b, 0)
        left_here(chosen_a, 4)

    @pl.when(core == 1)
    def _():
        left_here(spread_a, 0)
        left_here(spread_b.at[pl.ds(0, chip_count - 1)], 0)
        left_here(chosen_b, 4)

    far_push.wait_send()
    left_here(grad_ref.at[pl.ds(0, chip_count - 1)], 2)
    left_here(routed.at[pl.ds(0, fsdp_count - 1)], 5)
    left_here(out_rows.at[pl.ds(0, chip_count - 1), 0], 7)


def body(gradients, old_stats, stat_slot):
    fsdp_count = lax.axis_size("fsdp")
    chip_count = fsdp_count // 2
    blk_count, row_count, width = gradients.shape
    stat_count = stat_slot.shape[0]
    side = width // SPLIT
    parts = SPLIT * (SPLIT + 1) // 2 * (side // row_count) // chip_count
    parts_a, parts_b = parts - parts // 2, parts // 2
    square = (width, width)
    piece = (row_count, side)
    vmem = pltpu.VMEM
    return pl.pallas_call(
        kernel,
        out_shape=(
            jax.ShapeDtypeStruct(gradients.shape, gradients.dtype),
            jax.ShapeDtypeStruct(old_stats.shape, old_stats.dtype),
        ),
        in_specs=[pl.BlockSpec(memory_space=pl.ANY)] * 3,
        out_specs=(pl.BlockSpec(memory_space=pl.ANY), pl.BlockSpec(memory_space=pl.ANY)),
        scratch_shapes=[
            pltpu.SMEM((1, stat_count), jnp.int32),
            vmem((1, stat_count), jnp.int32),
            vmem((1, stat_count), jnp.int32),
            pltpu.SMEM((1, stat_count), jnp.int32),
            vmem((CAPS, *square), F32),
            vmem((chip_count, CAPS, parts_a, *piece), BF16),
            vmem((chip_count, CAPS, parts_b, *piece), BF16),
            vmem((fsdp_count, CAPS, parts_a, *piece), BF16),
            vmem((fsdp_count, CAPS, parts_b, *piece), BF16),
            vmem((fsdp_count, parts_a, *piece), BF16),
            vmem((fsdp_count, parts_b, *piece), BF16),
            vmem((chip_count, parts, *piece), BF16),
            vmem((blk_count, row_count, width), BF16),
            vmem((chip_count, 2, row_count, width), BF16),
            vmem((fsdp_count, CAPS, row_count, width), BF16),
            vmem((fsdp_count, CAPS, row_count, width), BF16),
            vmem((2, *square), BF16),
            vmem(square, F32),
            vmem(square, BF16),
            vmem(square, BF16),
            vmem(square, BF16),
            vmem(square, F32),
            vmem((chip_count, 2, row_count, width), BF16),
            pltpu.SemaphoreType.DMA((CAPS,)),
            pltpu.SemaphoreType.DMA((2,)),
            pltpu.SemaphoreType.DMA((8,)),
            pltpu.SemaphoreType.DMA((8,)),
        ],
        compiler_params=pltpu.CompilerParams(
            collective_id=0, has_side_effects=True, vmem_limit_bytes=60 * 2**20
        ),
        cost_estimate=pl.CostEstimate(
            flops=60 * width**3, bytes_accessed=5 * 2**20, transcendentals=0
        ),
    )(stat_slot.reshape(1, stat_count), gradients, old_stats)


def solution(mesh):
    return jax.shard_map(
        body,
        mesh=mesh,
        in_specs=(P("own", "fsdp", None), P(("fsdp", "own"), None, None), P()),
        out_specs=(P("own", "fsdp", None), P(("fsdp", "own"), None, None)),
        check_vma=False,
    )
```

```python
import math

import jax
import jax.numpy as jnp
from jax import lax
from jax.experimental import pallas as pl
from jax.experimental.pallas import tpu as pltpu
from jax.sharding import PartitionSpec as P

ITERS = 6
CAPS = 2
SPLIT = 4

keep_weight = 0.9
fresh_weight = 0.1
graft_eps = 1e-06

MESH = pl.DeviceIdType.MESH
BF16 = jnp.bfloat16
F32 = jnp.float32


def product(left_side, right_side):
    return jnp.dot(left_side, right_side, preferred_element_type=F32)


def rows_gram(block):
    return lax.dot_general(block, block, (((1,), (1,)), ((), ())), preferred_element_type=F32)


def columns_gram(block):
    return lax.dot_general(block, block, (((0,), (0,)), ((), ())), preferred_element_type=F32)


def total(values):
    return jnp.sum(jnp.sum(values, axis=0, keepdims=True), axis=1, keepdims=True)


def diagonal_mask(width):
    rows = lax.broadcasted_iota(jnp.int32, (width, width), 0)
    return rows == lax.broadcasted_iota(jnp.int32, (width, width), 1)


def upper_blocks(width):
    side = width // SPLIT
    pairs = [(i, j) for i in range(SPLIT) for j in range(i, SPLIT)]
    return side, [(pl.ds(i * side, side), pl.ds(j * side, side)) for i, j in pairs]


def kernel(
    slot_ref, grad_ref, old_ref,
    update_ref, new_ref,
    slots, slot_row, table_row, table,
    old_wide, spread_a, spread_b, gathered_a, gathered_b, chosen_a, chosen_b, old_rows,
    far_rows, block_rows, routed, routed_in, roots,
    moment, moment_low, gap_low, mixed_low, inverse, out_rows,
    load_sem, small_sem, send_sems, recv_sems,
):
    chip_count = spread_a.shape[0]
    fsdp_count = 2 * chip_count
    chip_side = math.isqrt(chip_count)
    own_count = lax.axis_size("own")
    row_count, width = grad_ref.shape[1:]
    stat_count = slot_ref.shape[1]
    f = lax.axis_index("fsdp")
    q = lax.axis_index("own")
    far = lax.rem(q + own_count // 2, own_count)
    core = lax.rem(f, 2)
    chip = f // 2
    sibling = f + 1 - 2 * core
    parts_a = spread_a.shape[2]
    parts_b = spread_b.shape[2]

    def chip_at(d):
        turn = lax.rem(5 * d, chip_count)
        y = lax.rem(chip // chip_side + turn // chip_side, chip_side)
        x = lax.rem(chip + turn, chip_side)
        return y * chip_side + x

    def push(src, dst, phase, row, plane):
        return pltpu.make_async_remote_copy(
            src_ref=src,
            dst_ref=dst,
            send_sem=send_sems.at[phase],
            recv_sem=recv_sems.at[phase],
            device_id={"fsdp": row, "own": plane},
            device_id_type=MESH,
        )

    def keep_here(src, dst, phase):
        pltpu.make_async_copy(src, dst, recv_sems.at[phase]).start()

    def arrived(ref, phase):
        pltpu.make_async_copy(ref, ref, recv_sems.at[phase]).wait()

    def left_here(ref, phase):
        pltpu.make_async_copy(ref, ref, send_sems.at[phase]).wait()

    loads = [
        pltpu.make_async_copy(old_ref.at[c], old_wide.at[c], load_sem.at[c]) for c in range(CAPS)
    ]
    slot_loads = [
        pltpu.make_async_copy(slot_ref, slots, small_sem.at[0]),
        pltpu.make_async_copy(slot_ref, slot_row, small_sem.at[1]),
    ]
    for load in loads + slot_loads:
        load.start()

    barrier = pltpu.get_barrier_semaphore()

    def greet(row, plane):
        pl.semaphore_signal(
            barrier, inc=1, device_id={"fsdp": row, "own": plane}, device_id_type=MESH
        )

    @pl.loop(1, fsdp_count)
    def _(d):
        greet(lax.rem(f + d, fsdp_count), q)

    greet(f, far)

    side, uppers = upper_blocks(width)
    pieces = side // row_count
    for c in range(CAPS):
        loads[c].wait()
        for b, (rows, columns) in enumerate(uppers):
            low = old_wide[c, rows, columns].astype(BF16).reshape(pieces, row_count, side)
            for piece in range(pieces):
                target, part = divmod(b * pieces + piece, parts_a + parts_b)
                if part < parts_a:
                    spread_a[target, c, part] = low[piece]
                else:
                    spread_b[target, c, part - parts_a] = low[piece]

    pl.semaphore_wait(barrier, fsdp_count)

    far_push = push(grad_ref, far_rows, 1, f, far)
    far_push.start()

    def spread_to(source, target, e):
        @pl.loop(1, chip_count)
        def _(d):
            t = chip_at(d)
            push(source.at[t], target.at[f], 0, 2 * t + e, q).start()

    @pl.when(core == 0)
    def _():
        spread_to(spread_a, gathered_a, 0)
        spread_to(spread_b, gathered_b, 1)
        push(spread_b.at[chip], gathered_b.at[f], 0, sibling, q).start()
        keep_here(spread_a.at[chip], gathered_a.at[f], 0)

    @pl.when(core == 1)
    def _():
        spread_to(spread_b, gathered_b, 1)
        spread_to(spread_a, gathered_a, 0)
        push(spread_a.at[chip], gathered_a.at[f], 0, sibling, q).start()
        keep_here(spread_b.at[chip], gathered_b.at[f], 0)

    @pl.loop(1, chip_count)
    def _(d):
        t = chip_at(d)
        push(grad_ref.at[t], block_rows.at[chip, core], 2, 2 * t + core, q).start()

    keep_here(grad_ref.at[chip], block_rows.at[chip, core], 2)

    for load in slot_loads:
        load.wait()
    grid = (stat_count, stat_count)
    by_stat = jnp.transpose(jnp.broadcast_to(slot_row[...], grid))
    place = jnp.right_shift(by_stat, 3) * CAPS + jnp.bitwise_and(by_stat, 1)
    here = jnp.bitwise_and(jnp.right_shift(by_stat, 1), 3) == q
    hit = here & (place == lax.broadcasted_iota(jnp.int32, grid, 1))
    names = lax.broadcasted_iota(jnp.int32, grid, 0) + 1
    table_row[...] = jnp.sum(jnp.where(hit, names, 0), axis=0, keepdims=True)
    table_copy = pltpu.make_async_copy(table_row, table, small_sem.at[0])
    table_copy.start()
    table_copy.wait()

    arrived(block_rows.at[:, core], 2)
    swap = push(block_rows.at[:, core], block_rows.at[:, core], 3, sibling, q)
    swap.start()

    far_push.wait_recv()

    @pl.loop(0, fsdp_count)
    def _(t):
        for c in range(CAPS):
            entry = lax.max(table[0, t * CAPS + c] - 1, 0)
            routed[t, c] = far_rows[lax.rem(entry, fsdp_count) // 2]

    def forward(gathered, chosen, first, parts):
        arrived(gathered, 0)

        @pl.loop(0, chip_count)
        def _(d):
            for e in range(2):
                t = 2 * chip_at(d) + e
                slot = slots[0, far * fsdp_count + t]
                chosen[t] = gathered[slot // (CAPS * own_count), lax.rem(slot, CAPS)]
                push(chosen.at[t], old_rows.at[chip, pl.ds(first, parts)], 4, t, far).start()

    @pl.when(core == 0)
    def _():
        forward(gathered_a, chosen_a, 0, parts_a)

    @pl.when(core == 1)
    def _():
        forward(gathered_b, chosen_b, parts_a, parts_b)

    @pl.loop(1, chip_count)
    def _(d):
        for e in range(2):
            t = 2 * chip_at(d) + e
            push(routed.at[t], routed_in.at[f], 5, t, q).start()

    push(routed.at[sibling], routed_in.at[f], 5, sibling, q).start()
    keep_here(routed.at[f], routed_in.at[f], 5)

    swap.wait()
    block = block_rows[...].reshape(width, width)
    wide = block.astype(F32)
    grad_total = total(wide * wide)

    @pl.when(core == 0)
    def _():
        moment[...] = rows_gram(block)

    @pl.when(core == 1)
    def _():
        moment[...] = columns_gram(block)

    arrived(old_rows, 4)
    on_diagonal = diagonal_mask(side)
    upper = old_rows[...].reshape(len(uppers), side, side)
    trace_value = jnp.zeros((1, 1), F32)
    for b, (rows, columns) in enumerate(uppers):
        old = keep_weight * upper[b].astype(F32)
        fresh = old + fresh_weight * moment[rows, columns]
        moment[rows, columns] = fresh
        if rows == columns:
            trace_value += total(jnp.where(on_diagonal, fresh, 0.0))
        else:
            moment[columns, rows] = jnp.transpose(fresh)
    start = moment[...] * (1.0 / trace_value)
    moment[...] = start
    moment_low[...] = start.astype(BF16)
    inverse[...] = -0.25 * start

    def sweep(step, level):
        low = moment_low[...]
        gap_low[...] = (product(low, low) - 10.0 * moment[...]).astype(BF16)
        mixed = (25.0 * moment[...] + product(gap_low[...], low)) * (1.0 / 16.0)
        mixed_low[...] = mixed.astype(BF16)
        fresh = (25.0 * mixed + product(gap_low[...], mixed_low[...])) * (1.0 / 16.0)
        moment[...] = fresh
        moment_low[...] = fresh.astype(BF16)
        inverse[...] = 1.25 * inverse[...] - 0.25 * (
            level * fresh + product(inverse[...].astype(BF16), moment_low[...])
        )
        return level * 1.25

    level = lax.fori_loop(0, ITERS - 1, sweep, jnp.float32(1.25))
    scale = 1.0 / jnp.sqrt(jnp.sqrt(trace_value))
    root = (jnp.where(diagonal_mask(width), level, 0.0) + inverse[...]) * scale
    roots[core] = root.astype(BF16)
    trade = push(roots.at[core], roots.at[core], 6, sibling, q)
    trade.start()
    trade.wait()

    hidden = product(roots[0], block).astype(BF16)
    shaped = product(hidden, roots[1])
    ratio = jnp.sqrt(grad_total / (total(shaped * shaped) + graft_eps))
    out_rows[...] = (shaped * ratio).astype(BF16).reshape(out_rows.shape)

    @pl.loop(1, chip_count)
    def _(d):
        t = chip_at(d)
        push(out_rows.at[t, core], update_ref.at[chip], 7, 2 * t + core, q).start()

    keep_here(out_rows.at[chip, core], update_ref.at[chip], 7)

    arrived(routed_in, 5)
    for c in range(CAPS):
        entry = table[0, f * CAPS + c]
        used = entry > 0
        odd = lax.rem(lax.max(entry - 1, 0), 2) == 1
        keep = jnp.where(used, keep_weight, 1.0)
        fresh = jnp.where(used, fresh_weight, 0.0)
        fresh_right = jnp.where(odd, fresh, 0.0)
        source = routed_in[:, c].reshape(width, width)
        gram = (fresh - fresh_right) * rows_gram(source) + fresh_right * columns_gram(source)
        new_ref[c] = keep * old_wide[c] + gram

    arrived(update_ref, 7)

    @pl.when(core == 0)
    def _():
        left_here(spread_a.at[pl.ds(0, chip_count - 1)], 0)
        left_here(spread_b, 0)
        left_here(chosen_a, 4)

    @pl.when(core == 1)
    def _():
        left_here(spread_a, 0)
        left_here(spread_b.at[pl.ds(0, chip_count - 1)], 0)
        left_here(chosen_b, 4)

    far_push.wait_send()
    left_here(grad_ref.at[pl.ds(0, chip_count - 1)], 2)
    left_here(routed.at[pl.ds(0, fsdp_count - 1)], 5)
    left_here(out_rows.at[pl.ds(0, chip_count - 1), 0], 7)


def write_out(update_ref, stats_ref, update_out, stats_out, sems):
    copies = [pltpu.make_async_copy(update_ref, update_out, sems.at[CAPS])]
    for c in range(CAPS):
        copies.append(pltpu.make_async_copy(stats_ref.at[c], stats_out.at[c], sems.at[c]))
    for copy in copies:
        copy.start()
    for copy in copies:
        copy.wait()


def body(gradients, old_stats, stat_slot):
    fsdp_count = lax.axis_size("fsdp")
    chip_count = fsdp_count // 2
    blk_count, row_count, width = gradients.shape
    stat_count = stat_slot.shape[0]
    side = width // SPLIT
    parts = SPLIT * (SPLIT + 1) // 2 * (side // row_count) // chip_count
    parts_a, parts_b = parts - parts // 2, parts // 2
    square = (width, width)
    piece = (row_count, side)
    vmem = pltpu.VMEM
    update, new_stats = pl.pallas_call(
        kernel,
        out_shape=(
            pltpu.VMEM(gradients.shape, gradients.dtype),
            pltpu.VMEM(old_stats.shape, old_stats.dtype),
        ),
        in_specs=[pl.BlockSpec(memory_space=pltpu.HBM)] * 3,
        out_specs=(pl.BlockSpec(memory_space=pl.ANY), pl.BlockSpec(memory_space=pltpu.VMEM)),
        scratch_shapes=[
            pltpu.SMEM((1, stat_count), jnp.int32),
            vmem((1, stat_count), jnp.int32),
            vmem((1, stat_count), jnp.int32),
            pltpu.SMEM((1, stat_count), jnp.int32),
            vmem((CAPS, *square), F32),
            vmem((chip_count, CAPS, parts_a, *piece), BF16),
            vmem((chip_count, CAPS, parts_b, *piece), BF16),
            vmem((fsdp_count, CAPS, parts_a, *piece), BF16),
            vmem((fsdp_count, CAPS, parts_b, *piece), BF16),
            vmem((fsdp_count, parts_a, *piece), BF16),
            vmem((fsdp_count, parts_b, *piece), BF16),
            vmem((chip_count, parts, *piece), BF16),
            vmem((blk_count, row_count, width), BF16),
            vmem((chip_count, 2, row_count, width), BF16),
            vmem((fsdp_count, CAPS, row_count, width), BF16),
            vmem((fsdp_count, CAPS, row_count, width), BF16),
            vmem((2, *square), BF16),
            vmem(square, F32),
            vmem(square, BF16),
            vmem(square, BF16),
            vmem(square, BF16),
            vmem(square, F32),
            vmem((chip_count, 2, row_count, width), BF16),
            pltpu.SemaphoreType.DMA((CAPS,)),
            pltpu.SemaphoreType.DMA((2,)),
            pltpu.SemaphoreType.DMA((8,)),
            pltpu.SemaphoreType.DMA((8,)),
        ],
        compiler_params=pltpu.CompilerParams(
            collective_id=0, has_side_effects=True, vmem_limit_bytes=57 * 2**20
        ),
        cost_estimate=pl.CostEstimate(
            flops=60 * width**3, bytes_accessed=5 * 2**20, transcendentals=0
        ),
    )(stat_slot.reshape(1, stat_count), gradients, old_stats)
    return pl.pallas_call(
        write_out,
        out_shape=(
            jax.ShapeDtypeStruct(gradients.shape, gradients.dtype),
            jax.ShapeDtypeStruct(old_stats.shape, old_stats.dtype),
        ),
        in_specs=[pl.BlockSpec(memory_space=pltpu.VMEM)] * 2,
        out_specs=(pl.BlockSpec(memory_space=pltpu.HBM), pl.BlockSpec(memory_space=pltpu.HBM)),
        scratch_shapes=[pltpu.SemaphoreType.DMA((1 + CAPS,))],
        compiler_params=pltpu.CompilerParams(vmem_limit_bytes=2**20),
    )(update, new_stats)


def solution(mesh):
    return jax.shard_map(
        body,
        mesh=mesh,
        in_specs=(P("own", "fsdp", None), P(("fsdp", "own"), None, None), P()),
        out_specs=(P("own", "fsdp", None), P(("fsdp", "own"), None, None)),
        check_vma=False,
    )
```

```python
import math

import jax
import jax.numpy as jnp
from jax import lax
from jax.experimental import pallas as pl
from jax.experimental.pallas import tpu as pltpu
from jax.sharding import PartitionSpec as P

ITERS = 6
CAPS = 2
SPLIT = 4
EARLY = 4

keep_weight = 0.9
fresh_weight = 0.1
graft_eps = 1e-06

MESH = pl.DeviceIdType.MESH
BF16 = jnp.bfloat16
F32 = jnp.float32


def product(left_side, right_side):
    return jnp.dot(left_side, right_side, preferred_element_type=F32)


def rows_gram(block):
    return lax.dot_general(block, block, (((1,), (1,)), ((), ())), preferred_element_type=F32)


def columns_gram(block):
    return lax.dot_general(block, block, (((0,), (0,)), ((), ())), preferred_element_type=F32)


def total(values):
    return jnp.sum(jnp.sum(values, axis=0, keepdims=True), axis=1, keepdims=True)


def diagonal_mask(width):
    rows = lax.broadcasted_iota(jnp.int32, (width, width), 0)
    return rows == lax.broadcasted_iota(jnp.int32, (width, width), 1)


def upper_blocks(width):
    side = width // SPLIT
    pairs = [(i, j) for i in range(SPLIT) for j in range(i, SPLIT)]
    return side, [(pl.ds(i * side, side), pl.ds(j * side, side)) for i, j in pairs]


def kernel(
    slot_ref, grad_ref, old_ref,
    update_ref, new_ref,
    slots, slot_row, table_row, table,
    old_wide, spread_a, spread_b, gathered_a, gathered_b, chosen_a, chosen_b, old_rows,
    far_rows, block_rows, routed, routed_in, roots,
    moment, moment_low, gap_low, mixed_low, inverse, out_rows,
    load_sem, small_sem, send_sems, recv_sems,
):
    chip_count = spread_a.shape[0]
    fsdp_count = 2 * chip_count
    chip_side = math.isqrt(chip_count)
    own_count = lax.axis_size("own")
    row_count, width = grad_ref.shape[1:]
    stat_count = slot_ref.shape[1]
    f = lax.axis_index("fsdp")
    q = lax.axis_index("own")
    far = lax.rem(q + own_count // 2, own_count)
    core = lax.rem(f, 2)
    chip = f // 2
    sibling = f + 1 - 2 * core
    parts_a = spread_a.shape[2]
    parts_b = spread_b.shape[2]

    def chip_at(d):
        turn = lax.rem(5 * d, chip_count)
        y = lax.rem(chip // chip_side + turn // chip_side, chip_side)
        x = lax.rem(chip + turn, chip_side)
        return y * chip_side + x

    def push(src, dst, phase, row, plane):
        return pltpu.make_async_remote_copy(
            src_ref=src,
            dst_ref=dst,
            send_sem=send_sems.at[phase],
            recv_sem=recv_sems.at[phase],
            device_id={"fsdp": row, "own": plane},
            device_id_type=MESH,
        )

    def keep_here(src, dst, phase):
        pltpu.make_async_copy(src, dst, recv_sems.at[phase]).start()

    def arrived(ref, phase):
        pltpu.make_async_copy(ref, ref, recv_sems.at[phase]).wait()

    def left_here(ref, phase):
        pltpu.make_async_copy(ref, ref, send_sems.at[phase]).wait()

    loads = [
        pltpu.make_async_copy(old_ref.at[c], old_wide.at[c], load_sem.at[c]) for c in range(CAPS)
    ]
    slot_loads = [
        pltpu.make_async_copy(slot_ref, slots, small_sem.at[0]),
        pltpu.make_async_copy(slot_ref, slot_row, small_sem.at[1]),
    ]
    for load in loads + slot_loads:
        load.start()

    barrier = pltpu.get_barrier_semaphore()

    def greet(row, plane):
        pl.semaphore_signal(
            barrier, inc=1, device_id={"fsdp": row, "own": plane}, device_id_type=MESH
        )

    @pl.loop(1, fsdp_count)
    def _(d):
        greet(lax.rem(f + d, fsdp_count), q)

    greet(f, far)

    side, uppers = upper_blocks(width)
    pieces = side // row_count
    for c in range(CAPS):
        loads[c].wait()
        for b, (rows, columns) in enumerate(uppers):
            low = old_wide[c, rows, columns].astype(BF16).reshape(pieces, row_count, side)
            for piece in range(pieces):
                target, part = divmod(b * pieces + piece, parts_a + parts_b)
                if part < parts_a:
                    spread_a[target, c, part] = low[piece]
                else:
                    spread_b[target, c, part - parts_a] = low[piece]

    pl.semaphore_wait(barrier, fsdp_count)

    far_push = push(grad_ref, far_rows, 1, f, far)
    far_push.start()

    def spread_to(source, target, e):
        @pl.loop(1, chip_count)
        def _(d):
            t = chip_at(d)
            push(source.at[t], target.at[f], 0, 2 * t + e, q).start()

    @pl.when(core == 0)
    def _():
        spread_to(spread_a, gathered_a, 0)
        spread_to(spread_b, gathered_b, 1)
        push(spread_b.at[chip], gathered_b.at[f], 0, sibling, q).start()
        keep_here(spread_a.at[chip], gathered_a.at[f], 0)

    @pl.when(core == 1)
    def _():
        spread_to(spread_b, gathered_b, 1)
        spread_to(spread_a, gathered_a, 0)
        push(spread_a.at[chip], gathered_a.at[f], 0, sibling, q).start()
        keep_here(spread_b.at[chip], gathered_b.at[f], 0)

    @pl.loop(1, chip_count)
    def _(d):
        t = chip_at(d)
        push(grad_ref.at[t], block_rows.at[chip, core], 2, 2 * t + core, q).start()

    keep_here(grad_ref.at[chip], block_rows.at[chip, core], 2)

    for load in slot_loads:
        load.wait()
    grid = (stat_count, stat_count)
    by_stat = jnp.transpose(jnp.broadcast_to(slot_row[...], grid))
    place = jnp.right_shift(by_stat, 3) * CAPS + jnp.bitwise_and(by_stat, 1)
    here = jnp.bitwise_and(jnp.right_shift(by_stat, 1), 3) == q
    hit = here & (place == lax.broadcasted_iota(jnp.int32, grid, 1))
    names = lax.broadcasted_iota(jnp.int32, grid, 0) + 1
    table_row[...] = jnp.sum(jnp.where(hit, names, 0), axis=0, keepdims=True)
    table_copy = pltpu.make_async_copy(table_row, table, small_sem.at[0])
    table_copy.start()
    table_copy.wait()

    far_push.wait_recv()

    def forward(gathered, chosen, first, parts):
        arrived(gathered, 0)

        @pl.loop(0, chip_count)
        def _(d):
            for e in range(2):
                t = 2 * chip_at(d) + e
                slot = slots[0, far * fsdp_count + t]
                chosen[t] = gathered[slot // (CAPS * own_count), lax.rem(slot, CAPS)]
                push(chosen.at[t], old_rows.at[chip, pl.ds(first, parts)], 4, t, far).start()

    @pl.when(core == 0)
    def _():
        forward(gathered_a, chosen_a, 0, parts_a)

    @pl.when(core == 1)
    def _():
        forward(gathered_b, chosen_b, parts_a, parts_b)

    arrived(block_rows.at[:, core], 2)
    swap = push(block_rows.at[:, core], block_rows.at[:, core], 3, sibling, q)
    swap.start()

    @pl.loop(0, fsdp_count)
    def _(t):
        for c in range(CAPS):
            entry = lax.max(table[0, t * CAPS + c] - 1, 0)
            routed[t, c] = far_rows[lax.rem(entry, fsdp_count) // 2]

    def route(first, last):
        @pl.loop(first, last)
        def _(d):
            for e in range(2):
                t = 2 * chip_at(d) + e
                push(routed.at[t], routed_in.at[f], 5, t, q).start()

    route(1, 1 + EARLY)
    push(routed.at[sibling], routed_in.at[f], 5, sibling, q).start()
    keep_here(routed.at[f], routed_in.at[f], 5)

    swap.wait()
    block = block_rows[...].reshape(width, width)
    wide = block.astype(F32)
    grad_total = total(wide * wide)

    @pl.when(core == 0)
    def _():
        moment[...] = rows_gram(block)

    @pl.when(core == 1)
    def _():
        moment[...] = columns_gram(block)

    arrived(old_rows, 4)
    route(1 + EARLY, chip_count)
    on_diagonal = diagonal_mask(side)
    upper = old_rows[...].reshape(len(uppers), side, side)
    trace_value = jnp.zeros((1, 1), F32)
    for b, (rows, columns) in enumerate(uppers):
        old = keep_weight * upper[b].astype(F32)
        fresh = old + fresh_weight * moment[rows, columns]
        moment[rows, columns] = fresh
        if rows == columns:
            trace_value += total(jnp.where(on_diagonal, fresh, 0.0))
        else:
            moment[columns, rows] = jnp.transpose(fresh)
    start = moment[...] * (1.0 / trace_value)
    moment[...] = start
    moment_low[...] = start.astype(BF16)
    inverse[...] = -0.25 * start

    def sweep(step, level):
        low = moment_low[...]
        gap_low[...] = (product(low, low) - 10.0 * moment[...]).astype(BF16)
        mixed = (25.0 * moment[...] + product(gap_low[...], low)) * (1.0 / 16.0)
        mixed_low[...] = mixed.astype(BF16)
        fresh = (25.0 * mixed + product(gap_low[...], mixed_low[...])) * (1.0 / 16.0)
        moment[...] = fresh
        moment_low[...] = fresh.astype(BF16)
        inverse[...] = 1.25 * inverse[...] - 0.25 * (
            level * fresh + product(inverse[...].astype(BF16), moment_low[...])
        )
        return level * 1.25

    level = lax.fori_loop(0, ITERS - 1, sweep, jnp.float32(1.25))
    scale = 1.0 / jnp.sqrt(jnp.sqrt(trace_value))
    root = (jnp.where(diagonal_mask(width), level, 0.0) + inverse[...]) * scale
    roots[core] = root.astype(BF16)
    trade = push(roots.at[core], roots.at[core], 6, sibling, q)
    trade.start()
    trade.wait()

    hidden = product(roots[0], block).astype(BF16)
    shaped = product(hidden, roots[1])
    ratio = jnp.sqrt(grad_total / (total(shaped * shaped) + graft_eps))
    out_rows[...] = (shaped * ratio).astype(BF16).reshape(out_rows.shape)

    @pl.loop(1, chip_count)
    def _(d):
        t = chip_at(d)
        push(out_rows.at[t, core], update_ref.at[chip], 7, 2 * t + core, q).start()

    keep_here(out_rows.at[chip, core], update_ref.at[chip], 7)

    arrived(routed_in, 5)
    for c in range(CAPS):
        entry = table[0, f * CAPS + c]
        used = entry > 0
        odd = lax.rem(lax.max(entry - 1, 0), 2) == 1
        keep = jnp.where(used, keep_weight, 1.0)
        fresh = jnp.where(used, fresh_weight, 0.0)
        fresh_right = jnp.where(odd, fresh, 0.0)
        source = routed_in[:, c].reshape(width, width)
        gram = (fresh - fresh_right) * rows_gram(source) + fresh_right * columns_gram(source)
        new_ref[c] = keep * old_wide[c] + gram

    arrived(update_ref, 7)

    @pl.when(core == 0)
    def _():
        left_here(spread_a.at[pl.ds(0, chip_count - 1)], 0)
        left_here(spread_b, 0)
        left_here(chosen_a, 4)

    @pl.when(core == 1)
    def _():
        left_here(spread_a, 0)
        left_here(spread_b.at[pl.ds(0, chip_count - 1)], 0)
        left_here(chosen_b, 4)

    far_push.wait_send()
    left_here(grad_ref.at[pl.ds(0, chip_count - 1)], 2)
    left_here(routed.at[pl.ds(0, fsdp_count - 1)], 5)
    left_here(out_rows.at[pl.ds(0, chip_count - 1), 0], 7)


def write_out(update_ref, stats_ref, update_out, stats_out, sems):
    copies = [pltpu.make_async_copy(update_ref, update_out, sems.at[CAPS])]
    for c in range(CAPS):
        copies.append(pltpu.make_async_copy(stats_ref.at[c], stats_out.at[c], sems.at[c]))
    for copy in copies:
        copy.start()
    for copy in copies:
        copy.wait()


def body(gradients, old_stats, stat_slot):
    fsdp_count = lax.axis_size("fsdp")
    chip_count = fsdp_count // 2
    blk_count, row_count, width = gradients.shape
    stat_count = stat_slot.shape[0]
    side = width // SPLIT
    parts = SPLIT * (SPLIT + 1) // 2 * (side // row_count) // chip_count
    parts_a, parts_b = parts - parts // 2, parts // 2
    square = (width, width)
    piece = (row_count, side)
    vmem = pltpu.VMEM
    update, new_stats = pl.pallas_call(
        kernel,
        out_shape=(
            pltpu.VMEM(gradients.shape, gradients.dtype),
            pltpu.VMEM(old_stats.shape, old_stats.dtype),
        ),
        in_specs=[pl.BlockSpec(memory_space=pltpu.HBM)] * 3,
        out_specs=(pl.BlockSpec(memory_space=pl.ANY), pl.BlockSpec(memory_space=pltpu.VMEM)),
        scratch_shapes=[
            pltpu.SMEM((1, stat_count), jnp.int32),
            vmem((1, stat_count), jnp.int32),
            vmem((1, stat_count), jnp.int32),
            pltpu.SMEM((1, stat_count), jnp.int32),
            vmem((CAPS, *square), F32),
            vmem((chip_count, CAPS, parts_a, *piece), BF16),
            vmem((chip_count, CAPS, parts_b, *piece), BF16),
            vmem((fsdp_count, CAPS, parts_a, *piece), BF16),
            vmem((fsdp_count, CAPS, parts_b, *piece), BF16),
            vmem((fsdp_count, parts_a, *piece), BF16),
            vmem((fsdp_count, parts_b, *piece), BF16),
            vmem((chip_count, parts, *piece), BF16),
            vmem((blk_count, row_count, width), BF16),
            vmem((chip_count, 2, row_count, width), BF16),
            vmem((fsdp_count, CAPS, row_count, width), BF16),
            vmem((fsdp_count, CAPS, row_count, width), BF16),
            vmem((2, *square), BF16),
            vmem(square, F32),
            vmem(square, BF16),
            vmem(square, BF16),
            vmem(square, BF16),
            vmem(square, F32),
            vmem((chip_count, 2, row_count, width), BF16),
            pltpu.SemaphoreType.DMA((CAPS,)),
            pltpu.SemaphoreType.DMA((2,)),
            pltpu.SemaphoreType.DMA((8,)),
            pltpu.SemaphoreType.DMA((8,)),
        ],
        compiler_params=pltpu.CompilerParams(
            collective_id=0, has_side_effects=True, vmem_limit_bytes=57 * 2**20
        ),
        cost_estimate=pl.CostEstimate(
            flops=60 * width**3, bytes_accessed=5 * 2**20, transcendentals=0
        ),
    )(stat_slot.reshape(1, stat_count), gradients, old_stats)
    return pl.pallas_call(
        write_out,
        out_shape=(
            jax.ShapeDtypeStruct(gradients.shape, gradients.dtype),
            jax.ShapeDtypeStruct(old_stats.shape, old_stats.dtype),
        ),
        in_specs=[pl.BlockSpec(memory_space=pltpu.VMEM)] * 2,
        out_specs=(pl.BlockSpec(memory_space=pltpu.HBM), pl.BlockSpec(memory_space=pltpu.HBM)),
        scratch_shapes=[pltpu.SemaphoreType.DMA((1 + CAPS,))],
        compiler_params=pltpu.CompilerParams(vmem_limit_bytes=2**20),
    )(update, new_stats)


def solution(mesh):
    return jax.shard_map(
        body,
        mesh=mesh,
        in_specs=(P("own", "fsdp", None), P(("fsdp", "own"), None, None), P()),
        out_specs=(P("own", "fsdp", None), P(("fsdp", "own"), None, None)),
        check_vma=False,
    )
```

```python
import functools
import math

import jax
import jax.numpy as jnp
from jax import lax
from jax.experimental import pallas as pl
from jax.experimental.pallas import tpu as pltpu
from jax.sharding import PartitionSpec as P

ITERS = 6
CAPS = 2
SPLIT = 4
EARLY = 2
PLACES = [(0, 0, 0), (0, 0, 1), (0, 1, 0), (1, 0, 0), (1, 1, 0)]
STAGES = 2
FIRST = [0, 8]

keep_weight = 0.9
fresh_weight = 0.1
graft_eps = 1e-06

MESH = pl.DeviceIdType.MESH
BF16 = jnp.bfloat16
F32 = jnp.float32


def product(left_side, right_side):
    return jnp.dot(left_side, right_side, preferred_element_type=F32)


def rows_gram(block):
    return lax.dot_general(block, block, (((1,), (1,)), ((), ())), preferred_element_type=F32)


def columns_gram(block):
    return lax.dot_general(block, block, (((0,), (0,)), ((), ())), preferred_element_type=F32)


def total(values):
    return jnp.sum(jnp.sum(values, axis=0, keepdims=True), axis=1, keepdims=True)


def diagonal_mask(width):
    rows = lax.broadcasted_iota(jnp.int32, (width, width), 0)
    return rows == lax.broadcasted_iota(jnp.int32, (width, width), 1)


def upper_blocks(width):
    side = width // SPLIT
    pairs = [(i, j) for i in range(SPLIT) for j in range(i, SPLIT)]
    return side, [(pl.ds(i * side, side), pl.ds(j * side, side)) for i, j in pairs]


def kernel(
    slot_ref, grad_ref, old_ref,
    update_ref, new_ref,
    slots, slot_row, table_row, table,
    old_wide, spread, gathered, chosen, old_rows,
    grads, far_rows, block_rows, routed, routed_in, roots,
    moment, moment_low, gap_low, mixed_low, inverse, out_rows,
    load_sem, small_sem, entered, send_sems, recv_sems,
):
    chip_count = spread[0][0].shape[0]
    fsdp_count = 2 * chip_count
    chip_side = math.isqrt(chip_count)
    own_count = lax.axis_size("own")
    row_count, width = grad_ref.shape[1:]
    stat_count = slot_ref.shape[1]
    f = lax.axis_index("fsdp")
    q = lax.axis_index("own")
    far = lax.rem(q + own_count // 2, own_count)
    core = lax.rem(f, 2)
    chip = f // 2
    sibling = f + 1 - 2 * core

    def chip_at(d):
        turn = lax.rem(5 * d, chip_count)
        y = lax.rem(chip // chip_side + turn // chip_side, chip_side)
        x = lax.rem(chip + turn, chip_side)
        return y * chip_side + x

    def push(src, dst, phase, row, plane):
        return pltpu.make_async_remote_copy(
            src_ref=src,
            dst_ref=dst,
            send_sem=send_sems.at[phase],
            recv_sem=recv_sems.at[phase],
            device_id={"fsdp": row, "own": plane},
            device_id_type=MESH,
        )

    def keep_here(src, dst, phase):
        pltpu.make_async_copy(src, dst, recv_sems.at[phase]).start()

    def arrived(ref, phase):
        pltpu.make_async_copy(ref, ref, recv_sems.at[phase]).wait()

    def left_here(ref, phase):
        pltpu.make_async_copy(ref, ref, send_sems.at[phase]).wait()

    loads = [
        pltpu.make_async_copy(old_ref.at[c], old_wide.at[c], load_sem.at[c]) for c in range(CAPS)
    ]
    slot_loads = [
        pltpu.make_async_copy(slot_ref, slots, small_sem.at[0]),
        pltpu.make_async_copy(slot_ref, slot_row, small_sem.at[1]),
    ]
    grad_load = pltpu.make_async_copy(grad_ref, grads, small_sem.at[2])
    for load in [*loads, grad_load, *slot_loads]:
        load.start()

    barrier = pltpu.get_barrier_semaphore()

    def greet(row, plane):
        pl.semaphore_signal(
            barrier, inc=1, device_id={"fsdp": row, "own": plane}, device_id_type=MESH
        )

    @pl.loop(1, fsdp_count)
    def _(d):
        greet(lax.rem(f + d, fsdp_count), q)

    greet(f, far)

    side, uppers = upper_blocks(width)
    pieces = side // row_count
    for c in range(CAPS):
        loads[c].wait()
        for b, (rows, columns) in enumerate(uppers):
            low = old_wide[c, rows, columns].astype(BF16).reshape(pieces, row_count, side)
            for piece in range(pieces):
                target, part = divmod(b * pieces + piece, len(PLACES))
                stage, e, at = PLACES[part]
                spread[stage][e][target, c, at] = low[piece]

    grad_load.wait()
    pl.semaphore_wait(barrier, fsdp_count)
    pl.semaphore_signal(
        entered, inc=1, device_id={"fsdp": f, "own": far}, device_id_type=MESH
    )

    far_push = push(grads, far_rows, 1, f, far)
    far_push.start()

    def spread_to(stage, e):
        source, target = spread[stage][e], gathered[stage][e]

        @pl.loop(1, chip_count)
        def _(d):
            t = chip_at(d)
            push(source.at[t], target.at[f], FIRST[stage], 2 * t + e, q).start()

    def spread_stage(stage, e):
        spread_to(stage, e)
        spread_to(stage, 1 - e)
        other = gathered[stage][1 - e]
        push(spread[stage][1 - e].at[chip], other.at[f], FIRST[stage], sibling, q).start()
        keep_here(spread[stage][e].at[chip], gathered[stage][e].at[f], FIRST[stage])

    for stage in range(STAGES):
        for e in range(2):
            pl.when(core == e)(functools.partial(spread_stage, stage, e))

    for load in slot_loads:
        load.wait()
    grid = (stat_count, stat_count)
    by_stat = jnp.transpose(jnp.broadcast_to(slot_row[...], grid))
    place = jnp.right_shift(by_stat, 3) * CAPS + jnp.bitwise_and(by_stat, 1)
    here = jnp.bitwise_and(jnp.right_shift(by_stat, 1), 3) == q
    hit = here & (place == lax.broadcasted_iota(jnp.int32, grid, 1))
    names = lax.broadcasted_iota(jnp.int32, grid, 0) + 1
    table_row[...] = jnp.sum(jnp.where(hit, names, 0), axis=0, keepdims=True)
    table_copy = pltpu.make_async_copy(table_row, table, small_sem.at[0])
    table_copy.start()
    table_copy.wait()

    pl.semaphore_wait(entered, 1)

    def forward(stage, e):
        source, picked = gathered[stage][e], chosen[stage][e]
        first, parts = PLACES.index((stage, e, 0)), picked.shape[1]
        arrived(source, FIRST[stage])

        @pl.loop(0, chip_count)
        def _(d):
            for side_core in range(2):
                t = 2 * chip_at(d) + side_core
                slot = slots[0, far * fsdp_count + t]
                picked[t] = source[slot // (CAPS * own_count), lax.rem(slot, CAPS)]
                push(picked.at[t], old_rows.at[chip, pl.ds(first, parts)], 4, t, far).start()

    for stage in range(STAGES):
        for e in range(2):
            pl.when(core == e)(functools.partial(forward, stage, e))

    @pl.loop(1, chip_count)
    def _(d):
        t = chip_at(d)
        push(grads.at[t], block_rows.at[chip, core], 2, 2 * t + core, q).start()

    keep_here(grads.at[chip], block_rows.at[chip, core], 2)

    arrived(block_rows.at[:, core], 2)
    swap = push(block_rows.at[:, core], block_rows.at[:, core], 3, sibling, q)
    swap.start()

    far_push.wait_recv()

    @pl.loop(0, fsdp_count)
    def _(t):
        for c in range(CAPS):
            entry = lax.max(table[0, t * CAPS + c] - 1, 0)
            routed[t, c] = far_rows[lax.rem(entry, fsdp_count) // 2]

    def route(first, last):
        @pl.loop(first, last)
        def _(d):
            for e in range(2):
                t = 2 * chip_at(d) + e
                push(routed.at[t], routed_in.at[f], 5, t, q).start()

    route(1, 1 + EARLY)
    push(routed.at[sibling], routed_in.at[f], 5, sibling, q).start()
    keep_here(routed.at[f], routed_in.at[f], 5)

    swap.wait()
    block = block_rows[...].reshape(width, width)
    wide = block.astype(F32)
    grad_total = total(wide * wide)

    @pl.when(core == 0)
    def _():
        moment[...] = rows_gram(block)

    @pl.when(core == 1)
    def _():
        moment[...] = columns_gram(block)

    arrived(old_rows, 4)
    route(1 + EARLY, chip_count)
    on_diagonal = diagonal_mask(side)
    upper = old_rows[...].reshape(len(uppers), side, side)
    trace_value = jnp.zeros((1, 1), F32)
    for b, (rows, columns) in enumerate(uppers):
        old = keep_weight * upper[b].astype(F32)
        fresh = old + fresh_weight * moment[rows, columns]
        moment[rows, columns] = fresh
        if rows == columns:
            trace_value += total(jnp.where(on_diagonal, fresh, 0.0))
        else:
            moment[columns, rows] = jnp.transpose(fresh)
    start = moment[...] * (1.0 / trace_value)
    moment[...] = start
    moment_low[...] = start.astype(BF16)
    inverse[...] = -0.25 * start

    def sweep(step, level):
        low = moment_low[...]
        gap_low[...] = (product(low, low) - 10.0 * moment[...]).astype(BF16)
        mixed = (25.0 * moment[...] + product(gap_low[...], low)) * (1.0 / 16.0)
        mixed_low[...] = mixed.astype(BF16)
        fresh = (25.0 * mixed + product(gap_low[...], mixed_low[...])) * (1.0 / 16.0)
        moment[...] = fresh
        moment_low[...] = fresh.astype(BF16)
        inverse[...] = 1.25 * inverse[...] - 0.25 * (
            level * fresh + product(inverse[...].astype(BF16), moment_low[...])
        )
        return level * 1.25

    level = lax.fori_loop(0, ITERS - 1, sweep, jnp.float32(1.25))
    scale = 1.0 / jnp.sqrt(jnp.sqrt(trace_value))
    root = (jnp.where(diagonal_mask(width), level, 0.0) + inverse[...]) * scale
    roots[core] = root.astype(BF16)
    trade = push(roots.at[core], roots.at[core], 6, sibling, q)
    trade.start()
    trade.wait()

    hidden = product(roots[0], block).astype(BF16)
    shaped = product(hidden, roots[1])
    ratio = jnp.sqrt(grad_total / (total(shaped * shaped) + graft_eps))
    out_rows[...] = (shaped * ratio).astype(BF16).reshape(out_rows.shape)

    @pl.loop(1, chip_count)
    def _(d):
        t = chip_at(d)
        push(out_rows.at[t, core], update_ref.at[chip], 7, 2 * t + core, q).start()

    keep_here(out_rows.at[chip, core], update_ref.at[chip], 7)

    arrived(routed_in, 5)
    for c in range(CAPS):
        entry = table[0, f * CAPS + c]
        used = entry > 0
        odd = lax.rem(lax.max(entry - 1, 0), 2) == 1
        keep = jnp.where(used, keep_weight, 1.0)
        fresh = jnp.where(used, fresh_weight, 0.0)
        fresh_right = jnp.where(odd, fresh, 0.0)
        source = routed_in[:, c].reshape(width, width)
        gram = (fresh - fresh_right) * rows_gram(source) + fresh_right * columns_gram(source)
        new_ref[c] = keep * old_wide[c] + gram

    arrived(update_ref, 7)

    def all_left(stage, e):
        left_here(spread[stage][e].at[pl.ds(0, chip_count - 1)], FIRST[stage])
        left_here(spread[stage][1 - e], FIRST[stage])
        left_here(chosen[stage][e], 4)

    for stage in range(STAGES):
        for e in range(2):
            pl.when(core == e)(functools.partial(all_left, stage, e))

    far_push.wait_send()
    left_here(grads.at[pl.ds(0, chip_count - 1)], 2)
    left_here(routed.at[pl.ds(0, fsdp_count - 1)], 5)
    left_here(out_rows.at[pl.ds(0, chip_count - 1), 0], 7)


def write_out(update_ref, stats_ref, update_out, stats_out, sems):
    copies = [pltpu.make_async_copy(update_ref, update_out, sems.at[CAPS])]
    for c in range(CAPS):
        copies.append(pltpu.make_async_copy(stats_ref.at[c], stats_out.at[c], sems.at[c]))
    for copy in copies:
        copy.start()
    for copy in copies:
        copy.wait()


def body(gradients, old_stats, stat_slot):
    fsdp_count = lax.axis_size("fsdp")
    chip_count = fsdp_count // 2
    blk_count, row_count, width = gradients.shape
    stat_count = stat_slot.shape[0]
    side = width // SPLIT
    square = (width, width)
    piece = (row_count, side)
    vmem = pltpu.VMEM

    def staged(*lead):
        def of(stage, e):
            parts = sum(place[:2] == (stage, e) for place in PLACES)
            return vmem((*lead, parts, *piece), BF16)

        return [[of(stage, e) for e in range(2)] for stage in range(STAGES)]

    update, new_stats = pl.pallas_call(
        kernel,
        out_shape=(
            pltpu.VMEM(gradients.shape, gradients.dtype),
            pltpu.VMEM(old_stats.shape, old_stats.dtype),
        ),
        in_specs=[pl.BlockSpec(memory_space=pltpu.HBM)] * 3,
        out_specs=(pl.BlockSpec(memory_space=pl.ANY), pl.BlockSpec(memory_space=pltpu.VMEM)),
        scratch_shapes=[
            pltpu.SMEM((1, stat_count), jnp.int32),
            vmem((1, stat_count), jnp.int32),
            vmem((1, stat_count), jnp.int32),
            pltpu.SMEM((1, stat_count), jnp.int32),
            vmem((CAPS, *square), F32),
            staged(chip_count, CAPS),
            staged(fsdp_count, CAPS),
            staged(fsdp_count),
            vmem((chip_count, len(PLACES), *piece), BF16),
            vmem((blk_count, row_count, width), BF16),
            vmem((blk_count, row_count, width), BF16),
            vmem((chip_count, 2, row_count, width), BF16),
            vmem((fsdp_count, CAPS, row_count, width), BF16),
            vmem((fsdp_count, CAPS, row_count, width), BF16),
            vmem((2, *square), BF16),
            vmem(square, F32),
            vmem(square, BF16),
            vmem(square, BF16),
            vmem(square, BF16),
            vmem(square, F32),
            vmem((chip_count, 2, row_count, width), BF16),
            pltpu.SemaphoreType.DMA((CAPS,)),
            pltpu.SemaphoreType.DMA((3,)),
            pltpu.SemaphoreType.REGULAR,
            pltpu.SemaphoreType.DMA((9,)),
            pltpu.SemaphoreType.DMA((9,)),
        ],
        compiler_params=pltpu.CompilerParams(
            collective_id=0, has_side_effects=True, vmem_limit_bytes=57 * 2**20
        ),
        cost_estimate=pl.CostEstimate(
            flops=60 * width**3, bytes_accessed=5 * 2**20, transcendentals=0
        ),
    )(stat_slot.reshape(1, stat_count), gradients, old_stats)
    return pl.pallas_call(
        write_out,
        out_shape=(
            jax.ShapeDtypeStruct(gradients.shape, gradients.dtype),
            jax.ShapeDtypeStruct(old_stats.shape, old_stats.dtype),
        ),
        in_specs=[pl.BlockSpec(memory_space=pltpu.VMEM)] * 2,
        out_specs=(pl.BlockSpec(memory_space=pltpu.HBM), pl.BlockSpec(memory_space=pltpu.HBM)),
        scratch_shapes=[pltpu.SemaphoreType.DMA((1 + CAPS,))],
        compiler_params=pltpu.CompilerParams(vmem_limit_bytes=2**20),
    )(update, new_stats)


def solution(mesh):
    return jax.shard_map(
        body,
        mesh=mesh,
        in_specs=(P("own", "fsdp", None), P(("fsdp", "own"), None, None), P()),
        out_specs=(P("own", "fsdp", None), P(("fsdp", "own"), None, None)),
        check_vma=False,
    )
```

```python
import functools
import math

import jax
import jax.numpy as jnp
from jax import lax
from jax.experimental import pallas as pl
from jax.experimental.pallas import tpu as pltpu
from jax.sharding import PartitionSpec as P

ITERS = 6
CAPS = 2
SPLIT = 4
EARLY = 4
PLACES = [(0, 0, 0), (0, 0, 1), (0, 1, 0), (1, 0, 0), (1, 1, 0)]
STAGES = 2
FIRST = [0, 8]

keep_weight = 0.9
fresh_weight = 0.1
graft_eps = 1e-06

MESH = pl.DeviceIdType.MESH
BF16 = jnp.bfloat16
F32 = jnp.float32


def product(left_side, right_side):
    return jnp.dot(left_side, right_side, preferred_element_type=F32)


def rows_gram(block):
    return lax.dot_general(block, block, (((1,), (1,)), ((), ())), preferred_element_type=F32)


def columns_gram(block):
    return lax.dot_general(block, block, (((0,), (0,)), ((), ())), preferred_element_type=F32)


def total(values):
    return jnp.sum(jnp.sum(values, axis=0, keepdims=True), axis=1, keepdims=True)


def diagonal_mask(width):
    rows = lax.broadcasted_iota(jnp.int32, (width, width), 0)
    return rows == lax.broadcasted_iota(jnp.int32, (width, width), 1)


def upper_blocks(width):
    side = width // SPLIT
    pairs = [(i, j) for i in range(SPLIT) for j in range(i, SPLIT)]
    return side, [(pl.ds(i * side, side), pl.ds(j * side, side)) for i, j in pairs]


def kernel(
    slot_ref, grad_ref, old_ref,
    update_ref, new_ref,
    slots, slot_row, table_row, table,
    old_wide, spread, gathered, chosen, old_rows,
    grads, far_rows, block_rows, block_all, routed, routed_in, roots,
    moment, moment_low, gap_low, mixed, mixed_low, inverse, inverse_low, out_rows,
    load_sem, small_sem, entered, send_sems, recv_sems,
):
    chip_count = spread[0][0].shape[0]
    fsdp_count = 2 * chip_count
    chip_side = math.isqrt(chip_count)
    own_count = lax.axis_size("own")
    row_count, width = grad_ref.shape[1:]
    stat_count = slot_ref.shape[1]
    f = lax.axis_index("fsdp")
    q = lax.axis_index("own")
    far = lax.rem(q + own_count // 2, own_count)
    core = lax.rem(f, 2)
    chip = f // 2
    sibling = f + 1 - 2 * core

    def chip_at(d):
        turn = lax.rem(5 * d, chip_count)
        y = lax.rem(chip // chip_side + turn // chip_side, chip_side)
        x = lax.rem(chip + turn, chip_side)
        return y * chip_side + x

    def push(src, dst, phase, row, plane):
        return pltpu.make_async_remote_copy(
            src_ref=src,
            dst_ref=dst,
            send_sem=send_sems.at[phase],
            recv_sem=recv_sems.at[phase],
            device_id={"fsdp": row, "own": plane},
            device_id_type=MESH,
        )

    def keep_here(src, dst, phase):
        pltpu.make_async_copy(src, dst, recv_sems.at[phase]).start()

    def arrived(ref, phase):
        pltpu.make_async_copy(ref, ref, recv_sems.at[phase]).wait()

    def left_here(ref, phase):
        pltpu.make_async_copy(ref, ref, send_sems.at[phase]).wait()

    loads = [
        pltpu.make_async_copy(old_ref.at[c], old_wide.at[c], load_sem.at[c]) for c in range(CAPS)
    ]
    slot_loads = [
        pltpu.make_async_copy(slot_ref, slots, small_sem.at[0]),
        pltpu.make_async_copy(slot_ref, slot_row, small_sem.at[1]),
    ]
    grad_load = pltpu.make_async_copy(grad_ref, grads, small_sem.at[2])
    for load in [*loads, grad_load, *slot_loads]:
        load.start()

    barrier = pltpu.get_barrier_semaphore()

    def greet(row, plane):
        pl.semaphore_signal(
            barrier, inc=1, device_id={"fsdp": row, "own": plane}, device_id_type=MESH
        )

    @pl.loop(1, fsdp_count)
    def _(d):
        greet(lax.rem(f + d, fsdp_count), q)

    greet(f, far)

    side, uppers = upper_blocks(width)
    pieces = side // row_count
    for c in range(CAPS):
        loads[c].wait()
        for b, (rows, columns) in enumerate(uppers):
            low = old_wide[c, rows, columns].astype(BF16).reshape(pieces, row_count, side)
            for piece in range(pieces):
                target, part = divmod(b * pieces + piece, len(PLACES))
                stage, e, at = PLACES[part]
                spread[stage][e][target, c, at] = low[piece]

    grad_load.wait()
    pl.semaphore_wait(barrier, fsdp_count)
    pl.semaphore_signal(
        entered, inc=1, device_id={"fsdp": f, "own": far}, device_id_type=MESH
    )

    far_push = push(grads, far_rows, 1, f, far)
    far_push.start()

    def spread_to(stage, e):
        source, target = spread[stage][e], gathered[stage][e]

        @pl.loop(1, chip_count)
        def _(d):
            t = chip_at(d)
            push(source.at[t], target.at[f], FIRST[stage], 2 * t + e, q).start()

    def spread_stage(stage, e):
        spread_to(stage, e)
        spread_to(stage, 1 - e)
        other = gathered[stage][1 - e]
        push(spread[stage][1 - e].at[chip], other.at[f], FIRST[stage], sibling, q).start()
        keep_here(spread[stage][e].at[chip], gathered[stage][e].at[f], FIRST[stage])

    for stage in range(STAGES):
        for e in range(2):
            pl.when(core == e)(functools.partial(spread_stage, stage, e))

    for load in slot_loads:
        load.wait()
    grid = (stat_count, stat_count)
    by_stat = jnp.transpose(jnp.broadcast_to(slot_row[...], grid))
    place = jnp.right_shift(by_stat, 3) * CAPS + jnp.bitwise_and(by_stat, 1)
    here = jnp.bitwise_and(jnp.right_shift(by_stat, 1), 3) == q
    hit = here & (place == lax.broadcasted_iota(jnp.int32, grid, 1))
    names = lax.broadcasted_iota(jnp.int32, grid, 0) + 1
    table_row[...] = jnp.sum(jnp.where(hit, names, 0), axis=0, keepdims=True)
    table_copy = pltpu.make_async_copy(table_row, table, small_sem.at[0])
    table_copy.start()
    table_copy.wait()

    pl.semaphore_wait(entered, 1)

    def forward(stage, e):
        source, picked = gathered[stage][e], chosen[stage][e]
        first, parts = PLACES.index((stage, e, 0)), picked.shape[1]
        arrived(source, FIRST[stage])

        @pl.loop(0, chip_count)
        def _(d):
            for side_core in range(2):
                t = 2 * chip_at(d) + side_core
                slot = slots[0, far * fsdp_count + t]
                picked[t] = source[slot // (CAPS * own_count), lax.rem(slot, CAPS)]
                push(picked.at[t], old_rows.at[chip, pl.ds(first, parts)], 4, t, far).start()

    for stage in range(STAGES):
        for e in range(2):
            pl.when(core == e)(functools.partial(forward, stage, e))

    @pl.loop(1, chip_count)
    def _(d):
        t = chip_at(d)
        push(grads.at[t], block_rows.at[chip, core], 2, 2 * t + core, q).start()

    keep_here(grads.at[chip], block_rows.at[chip, core], 2)

    arrived(block_rows.at[:, core], 2)
    swap = push(block_rows.at[:, core], block_rows.at[:, core], 3, sibling, q)
    swap.start()

    far_push.wait_recv()

    @pl.loop(0, fsdp_count)
    def _(t):
        for c in range(CAPS):
            entry = lax.max(table[0, t * CAPS + c] - 1, 0)
            routed[t, c] = far_rows[lax.rem(entry, fsdp_count) // 2]

    def route(first, last):
        @pl.loop(first, last)
        def _(d):
            for e in range(2):
                t = 2 * chip_at(d) + e
                push(routed.at[t], routed_in.at[f], 5, t, q).start()

    route(1, 1 + EARLY)
    push(routed.at[sibling], routed_in.at[f], 5, sibling, q).start()
    keep_here(routed.at[f], routed_in.at[f], 5)

    swap.wait()
    block_all[...] = block_rows[...].reshape(width, width)
    block = block_all[...]
    wide = block.astype(F32)
    grad_total = total(wide * wide)

    @pl.when(core == 0)
    def _():
        moment[...] = rows_gram(block)

    @pl.when(core == 1)
    def _():
        moment[...] = columns_gram(block)

    arrived(old_rows, 4)
    route(1 + EARLY, chip_count)
    on_diagonal = diagonal_mask(side)
    upper = old_rows[...].reshape(len(uppers), side, side)
    trace_value = jnp.zeros((1, 1), F32)
    half = width // 2
    left_half, right_half = pl.ds(0, half), pl.ds(half, half)
    bands = [pl.ds(b * side, side) for b in range(SPLIT)]
    tiles = [(band, right_half) for band in bands[:2]]
    tiles += [(band, left_half) for band in bands[:2]]
    tiles += [(band, right_half) for band in bands[2:]]

    def put(ref, rows, columns, values):
        rounded = values.astype(BF16)
        ref[rows, columns] = rounded
        if rows.start < half and columns.start == half:
            ref[columns, rows] = jnp.transpose(rounded)

    for b, (rows, columns) in enumerate(uppers):
        old = keep_weight * upper[b].astype(F32)
        fresh = old + fresh_weight * moment[rows, columns]
        moment[rows, columns] = fresh
        if rows == columns:
            trace_value += total(jnp.where(on_diagonal, fresh, 0.0))
        elif rows.start // half == columns.start // half:
            moment[columns, rows] = jnp.transpose(fresh)
    inverse_trace = 1.0 / trace_value
    for rows, columns in tiles:
        start = moment[rows, columns] * inverse_trace
        moment[rows, columns] = start
        put(moment_low, rows, columns, start)
        inverse[rows, columns] = -0.25 * start
        put(inverse_low, rows, columns, -0.25 * start)

    def next_inverse(rows, columns, level):
        part = product(inverse_low[rows, :], moment_low[:, columns])
        return 1.25 * inverse[rows, columns] - 0.25 * (level * moment[rows, columns] + part)

    def sweep(with_inverse, step, level):
        for rows, columns in tiles:
            square = product(moment_low[rows, :], moment_low[:, columns])
            put(gap_low, rows, columns, square - 10.0 * moment[rows, columns])
            if with_inverse:
                inverse[rows, columns] = next_inverse(rows, columns, level)
        if with_inverse:
            for rows, columns in tiles:
                put(inverse_low, rows, columns, inverse[rows, columns])
        for rows, columns in tiles:
            part = product(gap_low[rows, :], moment_low[:, columns])
            values = (25.0 * moment[rows, columns] + part) * (1.0 / 16.0)
            mixed[rows, columns] = values
            put(mixed_low, rows, columns, values)
        for rows, columns in tiles:
            part = product(gap_low[rows, :], mixed_low[:, columns])
            values = (25.0 * mixed[rows, columns] + part) * (1.0 / 16.0)
            moment[rows, columns] = values
            put(moment_low, rows, columns, values)
        return level * 1.25 if with_inverse else level

    sweep(False, 0, None)
    level = lax.fori_loop(1, ITERS - 1, functools.partial(sweep, True), jnp.float32(1.25))
    scale = 1.0 / jnp.sqrt(jnp.sqrt(trace_value))
    own_root = roots.at[core]
    for rows, columns in tiles:
        root = next_inverse(rows, columns, level)
        if rows.start // half == columns.start // half:
            spots = [
                lax.broadcasted_iota(jnp.int32, (side, half), dim) for dim in range(2)
            ]
            diagonal = spots[1] - spots[0] == rows.start - columns.start
            root += jnp.where(diagonal, 1.25 * level, 0.0)
        put(own_root, rows, columns, root * scale)
    trade = push(own_root, own_root, 6, sibling, q)
    trade.start()

    pl.when(core == 1)(trade.wait_recv)
    quarters = [(rows, columns) for columns in (left_half, right_half) for rows in (left_half, right_half)]
    for rows, columns in quarters:
        hidden = product(roots[0, rows, :], block_all[:, columns])
        gap_low[rows, columns] = hidden.astype(BF16)
    pl.when(core == 0)(trade.wait_recv)
    shaped_total = jnp.zeros((1, 1), F32)
    for rows, columns in quarters:
        shaped = product(gap_low[rows, :], roots[1, :, columns])
        mixed[rows, columns] = shaped
        shaped_total += total(shaped * shaped)
    ratio = jnp.sqrt(grad_total / (shaped_total + graft_eps))
    out_rows[...] = (mixed[...] * ratio).astype(BF16).reshape(out_rows.shape)

    @pl.loop(1, chip_count)
    def _(d):
        t = chip_at(d)
        push(out_rows.at[t, core], update_ref.at[chip], 7, 2 * t + core, q).start()

    keep_here(out_rows.at[chip, core], update_ref.at[chip], 7)

    arrived(routed_in, 5)
    for c in range(CAPS):
        entry = table[0, f * CAPS + c]
        used = entry > 0
        odd = lax.rem(lax.max(entry - 1, 0), 2) == 1
        keep = jnp.where(used, keep_weight, 1.0)
        fresh = jnp.where(used, fresh_weight, 0.0)
        fresh_right = jnp.where(odd, fresh, 0.0)
        source = routed_in[:, c].reshape(width, width)
        gram = (fresh - fresh_right) * rows_gram(source) + fresh_right * columns_gram(source)
        new_ref[c] = keep * old_wide[c] + gram

    arrived(update_ref, 7)

    def all_left(stage, e):
        left_here(spread[stage][e].at[pl.ds(0, chip_count - 1)], FIRST[stage])
        left_here(spread[stage][1 - e], FIRST[stage])
        left_here(chosen[stage][e], 4)

    for stage in range(STAGES):
        for e in range(2):
            pl.when(core == e)(functools.partial(all_left, stage, e))

    far_push.wait_send()
    left_here(grads.at[pl.ds(0, chip_count - 1)], 2)
    left_here(routed.at[pl.ds(0, fsdp_count - 1)], 5)
    trade.wait_send()
    left_here(out_rows.at[pl.ds(0, chip_count - 1), 0], 7)


def write_out(update_ref, stats_ref, update_out, stats_out, sems):
    copies = [pltpu.make_async_copy(update_ref, update_out, sems.at[CAPS])]
    for c in range(CAPS):
        copies.append(pltpu.make_async_copy(stats_ref.at[c], stats_out.at[c], sems.at[c]))
    for copy in copies:
        copy.start()
    for copy in copies:
        copy.wait()


def body(gradients, old_stats, stat_slot):
    fsdp_count = lax.axis_size("fsdp")
    chip_count = fsdp_count // 2
    blk_count, row_count, width = gradients.shape
    stat_count = stat_slot.shape[0]
    side = width // SPLIT
    square = (width, width)
    piece = (row_count, side)
    vmem = pltpu.VMEM

    def staged(*lead):
        def of(stage, e):
            parts = sum(place[:2] == (stage, e) for place in PLACES)
            return vmem((*lead, parts, *piece), BF16)

        return [[of(stage, e) for e in range(2)] for stage in range(STAGES)]

    update, new_stats = pl.pallas_call(
        kernel,
        out_shape=(
            pltpu.VMEM(gradients.shape, gradients.dtype),
            pltpu.VMEM(old_stats.shape, old_stats.dtype),
        ),
        in_specs=[pl.BlockSpec(memory_space=pltpu.HBM)] * 3,
        out_specs=(pl.BlockSpec(memory_space=pl.ANY), pl.BlockSpec(memory_space=pltpu.VMEM)),
        scratch_shapes=[
            pltpu.SMEM((1, stat_count), jnp.int32),
            vmem((1, stat_count), jnp.int32),
            vmem((1, stat_count), jnp.int32),
            pltpu.SMEM((1, stat_count), jnp.int32),
            vmem((CAPS, *square), F32),
            staged(chip_count, CAPS),
            staged(fsdp_count, CAPS),
            staged(fsdp_count),
            vmem((chip_count, len(PLACES), *piece), BF16),
            vmem((blk_count, row_count, width), BF16),
            vmem((blk_count, row_count, width), BF16),
            vmem((chip_count, 2, row_count, width), BF16),
            vmem(square, BF16),
            vmem((fsdp_count, CAPS, row_count, width), BF16),
            vmem((fsdp_count, CAPS, row_count, width), BF16),
            vmem((2, *square), BF16),
            vmem(square, F32),
            vmem(square, BF16),
            vmem(square, BF16),
            vmem(square, F32),
            vmem(square, BF16),
            vmem(square, F32),
            vmem(square, BF16),
            vmem((chip_count, 2, row_count, width), BF16),
            pltpu.SemaphoreType.DMA((CAPS,)),
            pltpu.SemaphoreType.DMA((3,)),
            pltpu.SemaphoreType.REGULAR,
            pltpu.SemaphoreType.DMA((9,)),
            pltpu.SemaphoreType.DMA((9,)),
        ],
        compiler_params=pltpu.CompilerParams(
            collective_id=0, has_side_effects=True, vmem_limit_bytes=57 * 2**20
        ),
        cost_estimate=pl.CostEstimate(
            flops=60 * width**3, bytes_accessed=5 * 2**20, transcendentals=0
        ),
    )(stat_slot.reshape(1, stat_count), gradients, old_stats)
    return pl.pallas_call(
        write_out,
        out_shape=(
            jax.ShapeDtypeStruct(gradients.shape, gradients.dtype),
            jax.ShapeDtypeStruct(old_stats.shape, old_stats.dtype),
        ),
        in_specs=[pl.BlockSpec(memory_space=pltpu.VMEM)] * 2,
        out_specs=(pl.BlockSpec(memory_space=pltpu.HBM), pl.BlockSpec(memory_space=pltpu.HBM)),
        scratch_shapes=[pltpu.SemaphoreType.DMA((1 + CAPS,))],
        compiler_params=pltpu.CompilerParams(vmem_limit_bytes=2**20),
    )(update, new_stats)


def solution(mesh):
    return jax.shard_map(
        body,
        mesh=mesh,
        in_specs=(P("own", "fsdp", None), P(("fsdp", "own"), None, None), P()),
        out_specs=(P("own", "fsdp", None), P(("fsdp", "own"), None, None)),
        check_vma=False,
    )
```

```python
import functools
import math

import jax
import jax.numpy as jnp
from jax import lax
from jax.experimental import pallas as pl
from jax.experimental.pallas import tpu as pltpu
from jax.sharding import PartitionSpec as P

ITERS = 6
CAPS = 2
SPLIT = 4
EARLY = 4
PLACES = [(0, 0, 0), (0, 0, 1), (0, 1, 0), (1, 0, 0), (1, 1, 0)]
STAGES = 2
FIRST = [0, 8]

keep_weight = 0.9
fresh_weight = 0.1
graft_eps = 1e-06

MESH = pl.DeviceIdType.MESH
BF16 = jnp.bfloat16
F32 = jnp.float32


def product(left_side, right_side):
    return jnp.dot(left_side, right_side, preferred_element_type=F32)


def rows_gram(block):
    return lax.dot_general(block, block, (((1,), (1,)), ((), ())), preferred_element_type=F32)


def columns_gram(block):
    return lax.dot_general(block, block, (((0,), (0,)), ((), ())), preferred_element_type=F32)


def total(values):
    return jnp.sum(jnp.sum(values, axis=0, keepdims=True), axis=1, keepdims=True)


def diagonal_mask(width):
    rows = lax.broadcasted_iota(jnp.int32, (width, width), 0)
    return rows == lax.broadcasted_iota(jnp.int32, (width, width), 1)


def upper_blocks(width):
    side = width // SPLIT
    pairs = [(i, j) for i in range(SPLIT) for j in range(i, SPLIT)]
    return side, [(pl.ds(i * side, side), pl.ds(j * side, side)) for i, j in pairs]


def kernel(
    slot_ref, grad_ref, old_ref,
    update_ref, new_ref,
    slots, slot_row, table_row, table,
    old_wide, spread, gathered, chosen, old_rows,
    grads, far_rows, block_rows, block_all, routed, routed_in, roots,
    moment, moment_low, gap_low, mixed, mixed_low, inverse, inverse_low, out_rows,
    load_sem, small_sem, entered, send_sems, recv_sems,
):
    chip_count = spread[0][0].shape[0]
    fsdp_count = 2 * chip_count
    chip_side = math.isqrt(chip_count)
    own_count = lax.axis_size("own")
    row_count, width = grad_ref.shape[1:]
    stat_count = slot_ref.shape[1]
    f = lax.axis_index("fsdp")
    q = lax.axis_index("own")
    far = lax.rem(q + own_count // 2, own_count)
    core = lax.rem(f, 2)
    chip = f // 2
    sibling = f + 1 - 2 * core

    def chip_at(d):
        turn = lax.rem(7 * d, chip_count)
        y = lax.rem(chip // chip_side + turn // chip_side, chip_side)
        x = lax.rem(chip + turn, chip_side)
        return y * chip_side + x

    def push(src, dst, phase, row, plane):
        return pltpu.make_async_remote_copy(
            src_ref=src,
            dst_ref=dst,
            send_sem=send_sems.at[phase],
            recv_sem=recv_sems.at[phase],
            device_id={"fsdp": row, "own": plane},
            device_id_type=MESH,
        )

    def keep_here(src, dst, phase):
        pltpu.make_async_copy(src, dst, recv_sems.at[phase]).start()

    def arrived(ref, phase):
        pltpu.make_async_copy(ref, ref, recv_sems.at[phase]).wait()

    def left_here(ref, phase):
        pltpu.make_async_copy(ref, ref, send_sems.at[phase]).wait()

    loads = [
        pltpu.make_async_copy(old_ref.at[c], old_wide.at[c], load_sem.at[c]) for c in range(CAPS)
    ]
    slot_loads = [
        pltpu.make_async_copy(slot_ref, slots, small_sem.at[0]),
        pltpu.make_async_copy(slot_ref, slot_row, small_sem.at[1]),
    ]
    grad_load = pltpu.make_async_copy(grad_ref, grads, small_sem.at[2])
    for load in [*loads, grad_load, *slot_loads]:
        load.start()

    barrier = pltpu.get_barrier_semaphore()

    def greet(row, plane):
        pl.semaphore_signal(
            barrier, inc=1, device_id={"fsdp": row, "own": plane}, device_id_type=MESH
        )

    @pl.loop(1, fsdp_count, unroll=True)
    def _(d):
        greet(lax.rem(f + d, fsdp_count), q)

    greet(f, far)

    side, uppers = upper_blocks(width)
    pieces = side // row_count
    for c in range(CAPS):
        loads[c].wait()
        for b, (rows, columns) in enumerate(uppers):
            low = old_wide[c, rows, columns].astype(BF16).reshape(pieces, row_count, side)
            for piece in range(pieces):
                target, part = divmod(b * pieces + piece, len(PLACES))
                stage, e, at = PLACES[part]
                spread[stage][e][target, c, at] = low[piece]

    grad_load.wait()
    pl.semaphore_wait(barrier, fsdp_count)
    pl.semaphore_signal(
        entered, inc=1, device_id={"fsdp": f, "own": far}, device_id_type=MESH
    )

    far_push = push(grads, far_rows, 1, f, far)
    far_push.start()

    def spread_to(stage, e):
        source, target = spread[stage][e], gathered[stage][e]

        @pl.loop(1, chip_count, unroll=True)
        def _(d):
            t = chip_at(d)
            push(source.at[t], target.at[f], FIRST[stage], 2 * t + e, q).start()

    def spread_stage(stage, e):
        spread_to(stage, e)
        spread_to(stage, 1 - e)
        other = gathered[stage][1 - e]
        push(spread[stage][1 - e].at[chip], other.at[f], FIRST[stage], sibling, q).start()
        keep_here(spread[stage][e].at[chip], gathered[stage][e].at[f], FIRST[stage])

    for stage in range(STAGES):
        for e in range(2):
            pl.when(core == e)(functools.partial(spread_stage, stage, e))

    for load in slot_loads:
        load.wait()
    grid = (stat_count, stat_count)
    by_stat = jnp.transpose(jnp.broadcast_to(slot_row[...], grid))
    place = jnp.right_shift(by_stat, 3) * CAPS + jnp.bitwise_and(by_stat, 1)
    here = jnp.bitwise_and(jnp.right_shift(by_stat, 1), 3) == q
    hit = here & (place == lax.broadcasted_iota(jnp.int32, grid, 1))
    names = lax.broadcasted_iota(jnp.int32, grid, 0) + 1
    table_row[...] = jnp.sum(jnp.where(hit, names, 0), axis=0, keepdims=True)
    table_copy = pltpu.make_async_copy(table_row, table, small_sem.at[0])
    table_copy.start()
    table_copy.wait()

    pl.semaphore_wait(entered, 1)

    def forward(stage, e):
        source, picked = gathered[stage][e], chosen[stage][e]
        first, parts = PLACES.index((stage, e, 0)), picked.shape[1]
        arrived(source, FIRST[stage])

        @pl.loop(0, chip_count, unroll=4)
        def _(d):
            for side_core in range(2):
                t = 2 * chip_at(d) + side_core
                slot = slots[0, far * fsdp_count + t]
                picked[t] = source[slot // (CAPS * own_count), lax.rem(slot, CAPS)]
                push(picked.at[t], old_rows.at[chip, pl.ds(first, parts)], 4, t, far).start()

    for e in range(2):
        pl.when(core == e)(functools.partial(forward, 0, e))

    @pl.loop(1, chip_count, unroll=True)
    def _(d):
        t = chip_at(d)
        push(grads.at[t], block_rows.at[chip, core], 2, 2 * t + core, q).start()

    keep_here(grads.at[chip], block_rows.at[chip, core], 2)

    for stage in range(1, STAGES):
        for e in range(2):
            pl.when(core == e)(functools.partial(forward, stage, e))

    arrived(block_rows.at[:, core], 2)
    swap = push(block_rows.at[:, core], block_rows.at[:, core], 3, sibling, q)
    swap.start()

    far_push.wait_recv()

    @pl.loop(0, fsdp_count, unroll=4)
    def _(t):
        for c in range(CAPS):
            entry = lax.max(table[0, t * CAPS + c] - 1, 0)
            routed[t, c] = far_rows[lax.rem(entry, fsdp_count) // 2]

    def route(first, last):
        @pl.loop(first, last)
        def _(d):
            for e in range(2):
                t = 2 * chip_at(d) + e
                push(routed.at[t], routed_in.at[f], 5, t, q).start()

    route(1, 1 + EARLY)
    push(routed.at[sibling], routed_in.at[f], 5, sibling, q).start()
    keep_here(routed.at[f], routed_in.at[f], 5)

    swap.wait()
    block_all[...] = block_rows[...].reshape(width, width)
    block = block_all[...]
    wide = block.astype(F32)
    grad_total = total(wide * wide)

    @pl.when(core == 0)
    def _():
        moment[...] = rows_gram(block)

    @pl.when(core == 1)
    def _():
        moment[...] = columns_gram(block)

    arrived(old_rows, 4)
    route(1 + EARLY, chip_count)
    on_diagonal = diagonal_mask(side)
    upper = old_rows[...].reshape(len(uppers), side, side)
    trace_value = jnp.zeros((1, 1), F32)
    half = width // 2
    left_half, right_half = pl.ds(0, half), pl.ds(half, half)
    bands = [pl.ds(b * side, side) for b in range(SPLIT)]
    tiles = [(band, right_half) for band in bands[:2]]
    tiles += [(band, left_half) for band in bands[:2]]
    tiles += [(band, right_half) for band in bands[2:]]

    def put(ref, rows, columns, values):
        rounded = values.astype(BF16)
        ref[rows, columns] = rounded
        if rows.start < half and columns.start == half:
            ref[columns, rows] = jnp.transpose(rounded)

    for b, (rows, columns) in enumerate(uppers):
        old = keep_weight * upper[b].astype(F32)
        fresh = old + fresh_weight * moment[rows, columns]
        moment[rows, columns] = fresh
        if rows == columns:
            trace_value += total(jnp.where(on_diagonal, fresh, 0.0))
        elif rows.start // half == columns.start // half:
            moment[columns, rows] = jnp.transpose(fresh)
    inverse_trace = 1.0 / trace_value
    for rows, columns in tiles:
        start = moment[rows, columns] * inverse_trace
        moment[rows, columns] = start
        put(moment_low, rows, columns, start)
        inverse[rows, columns] = -0.25 * start
        put(inverse_low, rows, columns, -0.25 * start)

    def next_inverse(rows, columns, level):
        part = product(inverse_low[rows, :], moment_low[:, columns])
        return 1.25 * inverse[rows, columns] - 0.25 * (level * moment[rows, columns] + part)

    def sweep(with_inverse, step, level):
        for rows, columns in tiles:
            square = product(moment_low[rows, :], moment_low[:, columns])
            put(gap_low, rows, columns, square - 10.0 * moment[rows, columns])
            if with_inverse:
                inverse[rows, columns] = next_inverse(rows, columns, level)
        if with_inverse:
            for rows, columns in tiles:
                put(inverse_low, rows, columns, inverse[rows, columns])
        for rows, columns in tiles:
            part = product(gap_low[rows, :], moment_low[:, columns])
            values = (25.0 * moment[rows, columns] + part) * (1.0 / 16.0)
            mixed[rows, columns] = values
            put(mixed_low, rows, columns, values)
        for rows, columns in tiles:
            part = product(gap_low[rows, :], mixed_low[:, columns])
            values = (25.0 * mixed[rows, columns] + part) * (1.0 / 16.0)
            moment[rows, columns] = values
            put(moment_low, rows, columns, values)
        return level * 1.25 if with_inverse else level

    sweep(False, 0, None)
    level = lax.fori_loop(1, ITERS - 1, functools.partial(sweep, True), jnp.float32(1.25))
    scale = 1.0 / jnp.sqrt(jnp.sqrt(trace_value))
    own_root = roots.at[core]

    def trade_half(rows):
        push(own_root.at[rows], own_root.at[rows], 6, sibling, q).start()

    for rows, columns in tiles:
        root = next_inverse(rows, columns, level)
        if rows.start // half == columns.start // half:
            spots = [
                lax.broadcasted_iota(jnp.int32, (side, half), dim) for dim in range(2)
            ]
            diagonal = spots[1] - spots[0] == rows.start - columns.start
            root += jnp.where(diagonal, 1.25 * level, 0.0)
        put(own_root, rows, columns, root * scale)
        if (rows, columns) == tiles[3]:
            trade_half(left_half)
    trade = push(own_root, own_root, 6, sibling, q)
    trade_half(right_half)

    pl.when(core == 1)(trade.wait_recv)
    quarters = [(rows, columns) for columns in (left_half, right_half) for rows in (left_half, right_half)]
    for rows, columns in quarters:
        hidden = product(roots[0, rows, :], block_all[:, columns])
        gap_low[rows, columns] = hidden.astype(BF16)
    pl.when(core == 0)(trade.wait_recv)
    shaped_total = jnp.zeros((1, 1), F32)
    for rows, columns in quarters:
        shaped = product(gap_low[rows, :], roots[1, :, columns])
        mixed[rows, columns] = shaped
        shaped_total += total(shaped * shaped)
    ratio = jnp.sqrt(grad_total / (shaped_total + graft_eps))
    out_rows[...] = (mixed[...] * ratio).astype(BF16).reshape(out_rows.shape)

    @pl.loop(1, chip_count, unroll=True)
    def _(d):
        t = chip_at(d)
        push(out_rows.at[t, core], update_ref.at[chip], 7, 2 * t + core, q).start()

    keep_here(out_rows.at[chip, core], update_ref.at[chip], 7)

    arrived(routed_in, 5)
    for c in range(CAPS):
        entry = table[0, f * CAPS + c]
        used = entry > 0
        odd = lax.rem(lax.max(entry - 1, 0), 2) == 1
        keep = jnp.where(used, keep_weight, 1.0)
        fresh = jnp.where(used, fresh_weight, 0.0)
        fresh_right = jnp.where(odd, fresh, 0.0)
        source = routed_in[:, c].reshape(width, width)
        gram = (fresh - fresh_right) * rows_gram(source) + fresh_right * columns_gram(source)
        new_ref[c] = keep * old_wide[c] + gram

    arrived(update_ref, 7)

    def all_left(stage, e):
        left_here(spread[stage][e].at[pl.ds(0, chip_count - 1)], FIRST[stage])
        left_here(spread[stage][1 - e], FIRST[stage])
        left_here(chosen[stage][e], 4)

    for stage in range(STAGES):
        for e in range(2):
            pl.when(core == e)(functools.partial(all_left, stage, e))

    far_push.wait_send()
    left_here(grads.at[pl.ds(0, chip_count - 1)], 2)
    left_here(routed.at[pl.ds(0, fsdp_count - 1)], 5)
    trade.wait_send()
    left_here(out_rows.at[pl.ds(0, chip_count - 1), 0], 7)


def write_out(update_ref, stats_ref, update_out, stats_out, sems):
    copies = [pltpu.make_async_copy(update_ref, update_out, sems.at[CAPS])]
    for c in range(CAPS):
        copies.append(pltpu.make_async_copy(stats_ref.at[c], stats_out.at[c], sems.at[c]))
    for copy in copies:
        copy.start()
    for copy in copies:
        copy.wait()


def body(gradients, old_stats, stat_slot):
    fsdp_count = lax.axis_size("fsdp")
    chip_count = fsdp_count // 2
    blk_count, row_count, width = gradients.shape
    stat_count = stat_slot.shape[0]
    side = width // SPLIT
    square = (width, width)
    piece = (row_count, side)
    vmem = pltpu.VMEM

    def staged(*lead):
        def of(stage, e):
            parts = sum(place[:2] == (stage, e) for place in PLACES)
            return vmem((*lead, parts, *piece), BF16)

        return [[of(stage, e) for e in range(2)] for stage in range(STAGES)]

    update, new_stats = pl.pallas_call(
        kernel,
        out_shape=(
            pltpu.VMEM(gradients.shape, gradients.dtype),
            pltpu.VMEM(old_stats.shape, old_stats.dtype),
        ),
        in_specs=[pl.BlockSpec(memory_space=pltpu.HBM)] * 3,
        out_specs=(pl.BlockSpec(memory_space=pl.ANY), pl.BlockSpec(memory_space=pltpu.VMEM)),
        scratch_shapes=[
            pltpu.SMEM((1, stat_count), jnp.int32),
            vmem((1, stat_count), jnp.int32),
            vmem((1, stat_count), jnp.int32),
            pltpu.SMEM((1, stat_count), jnp.int32),
            vmem((CAPS, *square), F32),
            staged(chip_count, CAPS),
            staged(fsdp_count, CAPS),
            staged(fsdp_count),
            vmem((chip_count, len(PLACES), *piece), BF16),
            vmem((blk_count, row_count, width), BF16),
            vmem((blk_count, row_count, width), BF16),
            vmem((chip_count, 2, row_count, width), BF16),
            vmem(square, BF16),
            vmem((fsdp_count, CAPS, row_count, width), BF16),
            vmem((fsdp_count, CAPS, row_count, width), BF16),
            vmem((2, *square), BF16),
            vmem(square, F32),
            vmem(square, BF16),
            vmem(square, BF16),
            vmem(square, F32),
            vmem(square, BF16),
            vmem(square, F32),
            vmem(square, BF16),
            vmem((chip_count, 2, row_count, width), BF16),
            pltpu.SemaphoreType.DMA((CAPS,)),
            pltpu.SemaphoreType.DMA((3,)),
            pltpu.SemaphoreType.REGULAR,
            pltpu.SemaphoreType.DMA((9,)),
            pltpu.SemaphoreType.DMA((9,)),
        ],
        compiler_params=pltpu.CompilerParams(
            collective_id=0, has_side_effects=True, vmem_limit_bytes=57 * 2**20
        ),
        cost_estimate=pl.CostEstimate(
            flops=60 * width**3, bytes_accessed=5 * 2**20, transcendentals=0
        ),
    )(stat_slot.reshape(1, stat_count), gradients, old_stats)
    return pl.pallas_call(
        write_out,
        out_shape=(
            jax.ShapeDtypeStruct(gradients.shape, gradients.dtype),
            jax.ShapeDtypeStruct(old_stats.shape, old_stats.dtype),
        ),
        in_specs=[pl.BlockSpec(memory_space=pltpu.VMEM)] * 2,
        out_specs=(pl.BlockSpec(memory_space=pltpu.HBM), pl.BlockSpec(memory_space=pltpu.HBM)),
        scratch_shapes=[pltpu.SemaphoreType.DMA((1 + CAPS,))],
        compiler_params=pltpu.CompilerParams(vmem_limit_bytes=2**20),
    )(update, new_stats)


def solution(mesh):
    return jax.shard_map(
        body,
        mesh=mesh,
        in_specs=(P("own", "fsdp", None), P(("fsdp", "own"), None, None), P()),
        out_specs=(P("own", "fsdp", None), P(("fsdp", "own"), None, None)),
        check_vma=False,
    )
```

```python
import functools
import math

import jax
import jax.numpy as jnp
from jax import lax
from jax.experimental import pallas as pl
from jax.experimental.pallas import tpu as pltpu
from jax.sharding import PartitionSpec as P

ITERS = 6
CAPS = 2
SPLIT = 4
EARLY = 4
PLACES = [(0, 0, 0), (0, 0, 1), (0, 1, 0), (1, 0, 0), (1, 1, 0)]
STAGES = 2
FIRST = [0, 8]

keep_weight = 0.9
fresh_weight = 0.1
graft_eps = 1e-06

MESH = pl.DeviceIdType.MESH
BF16 = jnp.bfloat16
F32 = jnp.float32


def product(left_side, right_side):
    return jnp.dot(left_side, right_side, preferred_element_type=F32)


def rows_gram(block):
    return lax.dot_general(block, block, (((1,), (1,)), ((), ())), preferred_element_type=F32)


def columns_gram(block):
    return lax.dot_general(block, block, (((0,), (0,)), ((), ())), preferred_element_type=F32)


def total(values):
    return jnp.sum(jnp.sum(values, axis=0, keepdims=True), axis=1, keepdims=True)


def diagonal_mask(width):
    rows = lax.broadcasted_iota(jnp.int32, (width, width), 0)
    return rows == lax.broadcasted_iota(jnp.int32, (width, width), 1)


def upper_blocks(width):
    side = width // SPLIT
    pairs = [(i, j) for i in range(SPLIT) for j in range(i, SPLIT)]
    return side, [(pl.ds(i * side, side), pl.ds(j * side, side)) for i, j in pairs]


def kernel(
    slot_ref, grad_ref, old_ref,
    update_ref, new_ref,
    slots, slot_row, table_row, table,
    old_wide, spread, gathered, chosen, old_rows,
    grads, far_rows, block_rows, block_all, routed, routed_in, roots,
    moment, moment_low, gap_low, mixed, mixed_low, inverse, inverse_low, out_rows,
    load_sem, small_sem, entered, send_sems, recv_sems,
):
    chip_count = spread[0][0].shape[0]
    fsdp_count = 2 * chip_count
    chip_side = math.isqrt(chip_count)
    own_count = lax.axis_size("own")
    row_count, width = grad_ref.shape[1:]
    stat_count = slot_ref.shape[1]
    f = lax.axis_index("fsdp")
    q = lax.axis_index("own")
    far = lax.rem(q + own_count // 2, own_count)
    core = lax.rem(f, 2)
    chip = f // 2
    sibling = f + 1 - 2 * core

    def chip_at(d):
        turn = lax.rem(7 * d, chip_count)
        y = lax.rem(chip // chip_side + turn // chip_side, chip_side)
        x = lax.rem(chip + turn, chip_side)
        return y * chip_side + x

    def push(src, dst, phase, row, plane):
        return pltpu.make_async_remote_copy(
            src_ref=src,
            dst_ref=dst,
            send_sem=send_sems.at[phase],
            recv_sem=recv_sems.at[phase],
            device_id={"fsdp": row, "own": plane},
            device_id_type=MESH,
        )

    def keep_here(src, dst, phase):
        pltpu.make_async_copy(src, dst, recv_sems.at[phase]).start()

    def arrived(ref, phase):
        pltpu.make_async_copy(ref, ref, recv_sems.at[phase]).wait()

    def left_here(ref, phase):
        pltpu.make_async_copy(ref, ref, send_sems.at[phase]).wait()

    loads = [
        pltpu.make_async_copy(old_ref.at[c], old_wide.at[c], load_sem.at[c]) for c in range(CAPS)
    ]
    slot_loads = [
        pltpu.make_async_copy(slot_ref, slots, small_sem.at[0]),
        pltpu.make_async_copy(slot_ref, slot_row, small_sem.at[1]),
    ]
    grad_load = pltpu.make_async_copy(grad_ref, grads, small_sem.at[2])
    for load in [*loads, grad_load, *slot_loads]:
        load.start()

    barrier = pltpu.get_barrier_semaphore()

    def greet(row, plane):
        pl.semaphore_signal(
            barrier, inc=1, device_id={"fsdp": row, "own": plane}, device_id_type=MESH
        )

    @pl.loop(1, fsdp_count, unroll=True)
    def _(d):
        greet(lax.rem(f + d, fsdp_count), q)

    greet(f, far)

    side, uppers = upper_blocks(width)
    pieces = side // row_count
    def lay_out(wanted):
        for c in range(CAPS):
            for b, (rows, columns) in enumerate(uppers):
                for piece in range(pieces):
                    target, part = divmod(b * pieces + piece, len(PLACES))
                    stage, e, at = PLACES[part]
                    if stage == wanted:
                        some = pl.ds(rows.start + piece * row_count, row_count)
                        spread[stage][e][target, c, at] = old_wide[c, some, columns].astype(BF16)

    for load in loads:
        load.wait()
    lay_out(0)
    grad_load.wait()
    pl.semaphore_wait(barrier, fsdp_count)
    pl.semaphore_signal(
        entered, inc=1, device_id={"fsdp": f, "own": far}, device_id_type=MESH
    )

    far_push = push(grads, far_rows, 1, f, far)
    far_push.start()

    def spread_to(stage, e):
        source, target = spread[stage][e], gathered[stage][e]

        @pl.loop(1, chip_count, unroll=True)
        def _(d):
            t = chip_at(d)
            push(source.at[t], target.at[f], FIRST[stage], 2 * t + e, q).start()

    def spread_stage(stage, e):
        spread_to(stage, e)
        spread_to(stage, 1 - e)
        other = gathered[stage][1 - e]
        push(spread[stage][1 - e].at[chip], other.at[f], FIRST[stage], sibling, q).start()
        keep_here(spread[stage][e].at[chip], gathered[stage][e].at[f], FIRST[stage])

    for stage in range(STAGES):
        if stage > 0:
            lay_out(stage)
        for e in range(2):
            pl.when(core == e)(functools.partial(spread_stage, stage, e))

    for load in slot_loads:
        load.wait()
    grid = (stat_count, stat_count)
    by_stat = jnp.transpose(jnp.broadcast_to(slot_row[...], grid))
    place = jnp.right_shift(by_stat, 3) * CAPS + jnp.bitwise_and(by_stat, 1)
    here = jnp.bitwise_and(jnp.right_shift(by_stat, 1), 3) == q
    hit = here & (place == lax.broadcasted_iota(jnp.int32, grid, 1))
    names = lax.broadcasted_iota(jnp.int32, grid, 0) + 1
    table_row[...] = jnp.sum(jnp.where(hit, names, 0), axis=0, keepdims=True)
    table_copy = pltpu.make_async_copy(table_row, table, small_sem.at[0])
    table_copy.start()
    table_copy.wait()

    pl.semaphore_wait(entered, 1)

    def forward(stage, e):
        source, picked = gathered[stage][e], chosen[stage][e]
        first, parts = PLACES.index((stage, e, 0)), picked.shape[1]
        arrived(source, FIRST[stage])

        @pl.loop(0, chip_count, unroll=4)
        def _(d):
            for side_core in range(2):
                t = 2 * chip_at(d) + side_core
                slot = slots[0, far * fsdp_count + t]
                picked[t] = source[slot // (CAPS * own_count), lax.rem(slot, CAPS)]
                push(picked.at[t], old_rows.at[chip, pl.ds(first, parts)], 4, t, far).start()

    for e in range(2):
        pl.when(core == e)(functools.partial(forward, 0, e))

    @pl.loop(1, chip_count, unroll=True)
    def _(d):
        t = chip_at(d)
        push(grads.at[t], block_rows.at[chip, core], 2, 2 * t + core, q).start()

    keep_here(grads.at[chip], block_rows.at[chip, core], 2)

    for stage in range(1, STAGES):
        for e in range(2):
            pl.when(core == e)(functools.partial(forward, stage, e))

    arrived(block_rows.at[:, core], 2)
    swap = push(block_rows.at[:, core], block_rows.at[:, core], 3, sibling, q)
    swap.start()

    far_push.wait_recv()

    @pl.loop(0, fsdp_count, unroll=4)
    def _(t):
        for c in range(CAPS):
            entry = lax.max(table[0, t * CAPS + c] - 1, 0)
            routed[t, c] = far_rows[lax.rem(entry, fsdp_count) // 2]

    def route(first, last):
        @pl.loop(first, last)
        def _(d):
            for e in range(2):
                t = 2 * chip_at(d) + e
                push(routed.at[t], routed_in.at[f], 5, t, q).start()

    route(1, 1 + EARLY)
    push(routed.at[sibling], routed_in.at[f], 5, sibling, q).start()
    keep_here(routed.at[f], routed_in.at[f], 5)

    swap.wait()
    block_all[...] = block_rows[...].reshape(width, width)
    block = block_all[...]
    wide = block.astype(F32)
    grad_total = total(wide * wide)

    @pl.when(core == 0)
    def _():
        moment[...] = rows_gram(block)

    @pl.when(core == 1)
    def _():
        moment[...] = columns_gram(block)

    arrived(old_rows, 4)
    route(1 + EARLY, chip_count)
    on_diagonal = diagonal_mask(side)
    upper = old_rows[...].reshape(len(uppers), side, side)
    trace_value = jnp.zeros((1, 1), F32)
    half = width // 2
    left_half, right_half = pl.ds(0, half), pl.ds(half, half)
    bands = [pl.ds(b * side, side) for b in range(SPLIT)]
    tiles = [(band, right_half) for band in bands[:2]]
    tiles += [(band, left_half) for band in bands[:2]]
    tiles += [(band, right_half) for band in bands[2:]]

    def put(ref, rows, columns, values):
        rounded = values.astype(BF16)
        ref[rows, columns] = rounded
        if rows.start < half and columns.start == half:
            ref[columns, rows] = jnp.transpose(rounded)

    for b, (rows, columns) in enumerate(uppers):
        old = keep_weight * upper[b].astype(F32)
        fresh = old + fresh_weight * moment[rows, columns]
        moment[rows, columns] = fresh
        if rows == columns:
            trace_value += total(jnp.where(on_diagonal, fresh, 0.0))
        elif rows.start // half == columns.start // half:
            moment[columns, rows] = jnp.transpose(fresh)
    inverse_trace = 1.0 / trace_value
    for rows, columns in tiles:
        start = moment[rows, columns] * inverse_trace
        moment[rows, columns] = start
        put(moment_low, rows, columns, start)
        inverse[rows, columns] = -0.25 * start
        put(inverse_low, rows, columns, -0.25 * start)

    def next_inverse(rows, columns, level):
        part = product(inverse_low[rows, :], moment_low[:, columns])
        return 1.25 * inverse[rows, columns] - 0.25 * (level * moment[rows, columns] + part)

    def sweep(with_inverse, step, level):
        for rows, columns in tiles:
            square = product(moment_low[rows, :], moment_low[:, columns])
            put(gap_low, rows, columns, square - 10.0 * moment[rows, columns])
            if with_inverse:
                inverse[rows, columns] = next_inverse(rows, columns, level)
        if with_inverse:
            for rows, columns in tiles:
                put(inverse_low, rows, columns, inverse[rows, columns])
        for rows, columns in tiles:
            part = product(gap_low[rows, :], moment_low[:, columns])
            values = (25.0 * moment[rows, columns] + part) * (1.0 / 16.0)
            mixed[rows, columns] = values
            put(mixed_low, rows, columns, values)
        for rows, columns in tiles:
            part = product(gap_low[rows, :], mixed_low[:, columns])
            values = (25.0 * mixed[rows, columns] + part) * (1.0 / 16.0)
            moment[rows, columns] = values
            put(moment_low, rows, columns, values)
        return level * 1.25 if with_inverse else level

    sweep(False, 0, None)
    level = lax.fori_loop(1, ITERS - 1, functools.partial(sweep, True), jnp.float32(1.25))
    scale = 1.0 / jnp.sqrt(jnp.sqrt(trace_value))
    own_root = roots.at[core]

    def trade_half(rows):
        push(own_root.at[rows], own_root.at[rows], 6, sibling, q).start()

    for rows, columns in tiles:
        root = next_inverse(rows, columns, level)
        if rows.start // half == columns.start // half:
            spots = [
                lax.broadcasted_iota(jnp.int32, (side, half), dim) for dim in range(2)
            ]
            diagonal = spots[1] - spots[0] == rows.start - columns.start
            root += jnp.where(diagonal, 1.25 * level, 0.0)
        put(own_root, rows, columns, root * scale)
        if (rows, columns) == tiles[3]:
            trade_half(left_half)
    trade = push(own_root, own_root, 6, sibling, q)
    trade_half(right_half)

    pl.when(core == 1)(trade.wait_recv)
    quarters = [(rows, columns) for columns in (left_half, right_half) for rows in (left_half, right_half)]
    for rows, columns in quarters:
        hidden = product(roots[0, rows, :], block_all[:, columns])
        gap_low[rows, columns] = hidden.astype(BF16)
    pl.when(core == 0)(trade.wait_recv)
    shaped_total = jnp.zeros((1, 1), F32)
    for rows, columns in quarters:
        shaped = product(gap_low[rows, :], roots[1, :, columns])
        mixed[rows, columns] = shaped
        shaped_total += total(shaped * shaped)
    ratio = jnp.sqrt(grad_total / (shaped_total + graft_eps))
    out_rows[...] = (mixed[...] * ratio).astype(BF16).reshape(out_rows.shape)

    @pl.loop(1, chip_count, unroll=True)
    def _(d):
        t = chip_at(d)
        push(out_rows.at[t, core], update_ref.at[chip], 7, 2 * t + core, q).start()

    keep_here(out_rows.at[chip, core], update_ref.at[chip], 7)

    arrived(routed_in, 5)
    for c in range(CAPS):
        entry = table[0, f * CAPS + c]
        used = entry > 0
        odd = lax.rem(lax.max(entry - 1, 0), 2) == 1
        keep = jnp.where(used, keep_weight, 1.0)
        fresh = jnp.where(used, fresh_weight, 0.0)
        fresh_right = jnp.where(odd, fresh, 0.0)
        source = routed_in[:, c].reshape(width, width)
        gram = (fresh - fresh_right) * rows_gram(source) + fresh_right * columns_gram(source)
        new_ref[c] = keep * old_wide[c] + gram

    arrived(update_ref, 7)

    def all_left(stage, e):
        left_here(spread[stage][e].at[pl.ds(0, chip_count - 1)], FIRST[stage])
        left_here(spread[stage][1 - e], FIRST[stage])
        left_here(chosen[stage][e], 4)

    for stage in range(STAGES):
        for e in range(2):
            pl.when(core == e)(functools.partial(all_left, stage, e))

    far_push.wait_send()
    left_here(grads.at[pl.ds(0, chip_count - 1)], 2)
    left_here(routed.at[pl.ds(0, fsdp_count - 1)], 5)
    trade.wait_send()
    left_here(out_rows.at[pl.ds(0, chip_count - 1), 0], 7)


def write_out(update_ref, stats_ref, update_out, stats_out, sems):
    copies = [pltpu.make_async_copy(update_ref, update_out, sems.at[CAPS])]
    for c in range(CAPS):
        copies.append(pltpu.make_async_copy(stats_ref.at[c], stats_out.at[c], sems.at[c]))
    for copy in copies:
        copy.start()
    for copy in copies:
        copy.wait()


def body(gradients, old_stats, stat_slot):
    fsdp_count = lax.axis_size("fsdp")
    chip_count = fsdp_count // 2
    blk_count, row_count, width = gradients.shape
    stat_count = stat_slot.shape[0]
    side = width // SPLIT
    square = (width, width)
    piece = (row_count, side)
    vmem = pltpu.VMEM

    def staged(*lead):
        def of(stage, e):
            parts = sum(place[:2] == (stage, e) for place in PLACES)
            return vmem((*lead, parts, *piece), BF16)

        return [[of(stage, e) for e in range(2)] for stage in range(STAGES)]

    update, new_stats = pl.pallas_call(
        kernel,
        out_shape=(
            pltpu.VMEM(gradients.shape, gradients.dtype),
            pltpu.VMEM(old_stats.shape, old_stats.dtype),
        ),
        in_specs=[pl.BlockSpec(memory_space=pltpu.HBM)] * 3,
        out_specs=(pl.BlockSpec(memory_space=pl.ANY), pl.BlockSpec(memory_space=pltpu.VMEM)),
        scratch_shapes=[
            pltpu.SMEM((1, stat_count), jnp.int32),
            vmem((1, stat_count), jnp.int32),
            vmem((1, stat_count), jnp.int32),
            pltpu.SMEM((1, stat_count), jnp.int32),
            vmem((CAPS, *square), F32),
            staged(chip_count, CAPS),
            staged(fsdp_count, CAPS),
            staged(fsdp_count),
            vmem((chip_count, len(PLACES), *piece), BF16),
            vmem((blk_count, row_count, width), BF16),
            vmem((blk_count, row_count, width), BF16),
            vmem((chip_count, 2, row_count, width), BF16),
            vmem(square, BF16),
            vmem((fsdp_count, CAPS, row_count, width), BF16),
            vmem((fsdp_count, CAPS, row_count, width), BF16),
            vmem((2, *square), BF16),
            vmem(square, F32),
            vmem(square, BF16),
            vmem(square, BF16),
            vmem(square, F32),
            vmem(square, BF16),
            vmem(square, F32),
            vmem(square, BF16),
            vmem((chip_count, 2, row_count, width), BF16),
            pltpu.SemaphoreType.DMA((CAPS,)),
            pltpu.SemaphoreType.DMA((3,)),
            pltpu.SemaphoreType.REGULAR,
            pltpu.SemaphoreType.DMA((9,)),
            pltpu.SemaphoreType.DMA((9,)),
        ],
        compiler_params=pltpu.CompilerParams(
            collective_id=0, has_side_effects=True, vmem_limit_bytes=57 * 2**20
        ),
        cost_estimate=pl.CostEstimate(
            flops=60 * width**3, bytes_accessed=5 * 2**20, transcendentals=0
        ),
    )(stat_slot.reshape(1, stat_count), gradients, old_stats)
    return pl.pallas_call(
        write_out,
        out_shape=(
            jax.ShapeDtypeStruct(gradients.shape, gradients.dtype),
            jax.ShapeDtypeStruct(old_stats.shape, old_stats.dtype),
        ),
        in_specs=[pl.BlockSpec(memory_space=pltpu.VMEM)] * 2,
        out_specs=(pl.BlockSpec(memory_space=pltpu.HBM), pl.BlockSpec(memory_space=pltpu.HBM)),
        scratch_shapes=[pltpu.SemaphoreType.DMA((1 + CAPS,))],
        compiler_params=pltpu.CompilerParams(vmem_limit_bytes=2**20),
    )(update, new_stats)


def solution(mesh):
    return jax.shard_map(
        body,
        mesh=mesh,
        in_specs=(P("own", "fsdp", None), P(("fsdp", "own"), None, None), P()),
        out_specs=(P("own", "fsdp", None), P(("fsdp", "own"), None, None)),
        check_vma=False,
    )
```

```python
import functools
import math

import jax
import jax.numpy as jnp
from jax import lax
from jax.experimental import pallas as pl
from jax.experimental.pallas import tpu as pltpu
from jax.sharding import PartitionSpec as P

ITERS = 6
CAPS = 2
SPLIT = 4
EARLY = 6
PLACES = [(0, 0, 0), (0, 0, 1), (0, 1, 0), (1, 0, 0), (1, 1, 0)]
STAGES = 2
FIRST = [0, 8]

keep_weight = 0.9
fresh_weight = 0.1
graft_eps = 1e-06

MESH = pl.DeviceIdType.MESH
BF16 = jnp.bfloat16
F32 = jnp.float32


def product(left_side, right_side):
    return jnp.dot(left_side, right_side, preferred_element_type=F32)


def rows_gram(block):
    return lax.dot_general(block, block, (((1,), (1,)), ((), ())), preferred_element_type=F32)


def columns_gram(block):
    return lax.dot_general(block, block, (((0,), (0,)), ((), ())), preferred_element_type=F32)


def total(values):
    return jnp.sum(jnp.sum(values, axis=0, keepdims=True), axis=1, keepdims=True)


def diagonal_mask(width):
    rows = lax.broadcasted_iota(jnp.int32, (width, width), 0)
    return rows == lax.broadcasted_iota(jnp.int32, (width, width), 1)


def upper_blocks(width):
    side = width // SPLIT
    pairs = [(i, j) for i in range(SPLIT) for j in range(i, SPLIT)]
    return side, [(pl.ds(i * side, side), pl.ds(j * side, side)) for i, j in pairs]


def kernel(
    slot_ref, grad_ref, old_ref,
    update_ref, new_ref,
    slots, slot_row, table_row, table,
    old_wide, spread, gathered, chosen, old_rows,
    grads, far_rows, block_rows, block_all, routed, routed_in, roots,
    moment, moment_low, gap_low, mixed, mixed_low, inverse, inverse_low, out_rows,
    load_sem, small_sem, entered, send_sems, recv_sems,
):
    chip_count = spread[0][0].shape[0]
    fsdp_count = 2 * chip_count
    chip_side = math.isqrt(chip_count)
    own_count = lax.axis_size("own")
    row_count, width = grad_ref.shape[1:]
    stat_count = slot_ref.shape[1]
    f = lax.axis_index("fsdp")
    q = lax.axis_index("own")
    far = lax.rem(q + own_count // 2, own_count)
    core = lax.rem(f, 2)
    chip = f // 2
    sibling = f + 1 - 2 * core

    def chip_at(d):
        turn = lax.rem(7 * d, chip_count)
        y = lax.rem(chip // chip_side + turn // chip_side, chip_side)
        x = lax.rem(chip + turn, chip_side)
        return y * chip_side + x

    def push(src, dst, phase, row, plane):
        return pltpu.make_async_remote_copy(
            src_ref=src,
            dst_ref=dst,
            send_sem=send_sems.at[phase],
            recv_sem=recv_sems.at[phase],
            device_id={"fsdp": row, "own": plane},
            device_id_type=MESH,
        )

    def keep_here(src, dst, phase):
        pltpu.make_async_copy(src, dst, recv_sems.at[phase]).start()

    def arrived(ref, phase):
        pltpu.make_async_copy(ref, ref, recv_sems.at[phase]).wait()

    def left_here(ref, phase):
        pltpu.make_async_copy(ref, ref, send_sems.at[phase]).wait()

    loads = [
        pltpu.make_async_copy(old_ref.at[c], old_wide.at[c], load_sem.at[c]) for c in range(CAPS)
    ]
    slot_loads = [
        pltpu.make_async_copy(slot_ref, slots, small_sem.at[0]),
        pltpu.make_async_copy(slot_ref, slot_row, small_sem.at[1]),
    ]
    grad_load = pltpu.make_async_copy(grad_ref, grads, small_sem.at[2])
    for load in [*loads, grad_load, *slot_loads]:
        load.start()

    barrier = pltpu.get_barrier_semaphore()

    def greet(row, plane):
        pl.semaphore_signal(
            barrier, inc=1, device_id={"fsdp": row, "own": plane}, device_id_type=MESH
        )

    @pl.loop(1, fsdp_count, unroll=True)
    def _(d):
        greet(lax.rem(f + d, fsdp_count), q)

    greet(f, far)

    side, uppers = upper_blocks(width)
    pieces = side // row_count
    for c in range(CAPS):
        loads[c].wait()
        for b, (rows, columns) in enumerate(uppers):
            low = old_wide[c, rows, columns].astype(BF16).reshape(pieces, row_count, side)
            for piece in range(pieces):
                target, part = divmod(b * pieces + piece, len(PLACES))
                stage, e, at = PLACES[part]
                spread[stage][e][target, c, at] = low[piece]

    grad_load.wait()
    pl.semaphore_wait(barrier, fsdp_count)
    pl.semaphore_signal(
        entered, inc=1, device_id={"fsdp": f, "own": far}, device_id_type=MESH
    )

    far_push = push(grads, far_rows, 1, f, far)
    far_push.start()

    def spread_to(stage, e):
        source, target = spread[stage][e], gathered[stage][e]

        @pl.loop(1, chip_count, unroll=True)
        def _(d):
            t = chip_at(d)
            push(source.at[t], target.at[f], FIRST[stage], 2 * t + e, q).start()

    def spread_stage(stage, e):
        spread_to(stage, e)
        spread_to(stage, 1 - e)
        other = gathered[stage][1 - e]
        push(spread[stage][1 - e].at[chip], other.at[f], FIRST[stage], sibling, q).start()
        keep_here(spread[stage][e].at[chip], gathered[stage][e].at[f], FIRST[stage])

    for stage in range(STAGES):
        for e in range(2):
            pl.when(core == e)(functools.partial(spread_stage, stage, e))

    for load in slot_loads:
        load.wait()
    grid = (stat_count, stat_count)
    by_stat = jnp.transpose(jnp.broadcast_to(slot_row[...], grid))
    place = jnp.right_shift(by_stat, 3) * CAPS + jnp.bitwise_and(by_stat, 1)
    here = jnp.bitwise_and(jnp.right_shift(by_stat, 1), 3) == q
    hit = here & (place == lax.broadcasted_iota(jnp.int32, grid, 1))
    names = lax.broadcasted_iota(jnp.int32, grid, 0) + 1
    table_row[...] = jnp.sum(jnp.where(hit, names, 0), axis=0, keepdims=True)
    table_copy = pltpu.make_async_copy(table_row, table, small_sem.at[0])
    table_copy.start()
    table_copy.wait()

    pl.semaphore_wait(entered, 1)

    def forward(stage, e):
        source, picked = gathered[stage][e], chosen[stage][e]
        first, parts = PLACES.index((stage, e, 0)), picked.shape[1]
        arrived(source, FIRST[stage])

        @pl.loop(0, chip_count, unroll=4)
        def _(d):
            for side_core in range(2):
                t = 2 * chip_at(d) + side_core
                slot = slots[0, far * fsdp_count + t]
                picked[t] = source[slot // (CAPS * own_count), lax.rem(slot, CAPS)]
                push(picked.at[t], old_rows.at[chip, pl.ds(first, parts)], 4, t, far).start()

    for e in range(2):
        pl.when(core == e)(functools.partial(forward, 0, e))

    @pl.loop(1, chip_count, unroll=True)
    def _(d):
        t = chip_at(d)
        push(grads.at[t], block_rows.at[chip, core], 2, 2 * t + core, q).start()

    keep_here(grads.at[chip], block_rows.at[chip, core], 2)

    for stage in range(1, STAGES):
        for e in range(2):
            pl.when(core == e)(functools.partial(forward, stage, e))

    arrived(block_rows.at[:, core], 2)
    swap = push(block_rows.at[:, core], block_rows.at[:, core], 3, sibling, q)
    swap.start()

    far_push.wait_recv()

    @pl.loop(0, fsdp_count, unroll=4)
    def _(t):
        for c in range(CAPS):
            entry = lax.max(table[0, t * CAPS + c] - 1, 0)
            routed[t, c] = far_rows[lax.rem(entry, fsdp_count) // 2]

    def route(first, last):
        @pl.loop(first, last)
        def _(d):
            for e in range(2):
                t = 2 * chip_at(d) + e
                push(routed.at[t], routed_in.at[f], 5, t, q).start()

    route(1, 1 + EARLY)
    push(routed.at[sibling], routed_in.at[f], 5, sibling, q).start()
    keep_here(routed.at[f], routed_in.at[f], 5)

    swap.wait()
    block_all[...] = block_rows[...].reshape(width, width)
    block = block_all[...]
    wide = block.astype(F32)
    grad_total = total(wide * wide)

    @pl.when(core == 0)
    def _():
        moment[...] = rows_gram(block)

    @pl.when(core == 1)
    def _():
        moment[...] = columns_gram(block)

    arrived(old_rows, 4)
    route(1 + EARLY, chip_count)
    on_diagonal = diagonal_mask(side)
    upper = old_rows[...].reshape(len(uppers), side, side)
    trace_value = jnp.zeros((1, 1), F32)
    half = width // 2
    left_half, right_half = pl.ds(0, half), pl.ds(half, half)
    bands = [pl.ds(b * side, side) for b in range(SPLIT)]
    tiles = [(band, right_half) for band in bands[:2]]
    tiles += [(band, left_half) for band in bands[:2]]
    tiles += [(band, right_half) for band in bands[2:]]

    def put(ref, rows, columns, values):
        rounded = values.astype(BF16)
        ref[rows, columns] = rounded
        if rows.start < half and columns.start == half:
            ref[columns, rows] = jnp.transpose(rounded)

    for b, (rows, columns) in enumerate(uppers):
        old = keep_weight * upper[b].astype(F32)
        fresh = old + fresh_weight * moment[rows, columns]
        moment[rows, columns] = fresh
        if rows == columns:
            trace_value += total(jnp.where(on_diagonal, fresh, 0.0))
        elif rows.start // half == columns.start // half:
            moment[columns, rows] = jnp.transpose(fresh)
    inverse_trace = 1.0 / trace_value
    for rows, columns in tiles:
        start = moment[rows, columns] * inverse_trace
        moment[rows, columns] = start
        put(moment_low, rows, columns, start)
        inverse[rows, columns] = -0.25 * start
        put(inverse_low, rows, columns, -0.25 * start)

    def next_inverse(rows, columns, level):
        part = product(inverse_low[rows, :], moment_low[:, columns])
        return 1.25 * inverse[rows, columns] - 0.25 * (level * moment[rows, columns] + part)

    def sweep(with_inverse, step, level):
        for rows, columns in tiles:
            square = product(moment_low[rows, :], moment_low[:, columns])
            put(gap_low, rows, columns, square - 10.0 * moment[rows, columns])
            if with_inverse:
                inverse[rows, columns] = next_inverse(rows, columns, level)
        if with_inverse:
            for rows, columns in tiles:
                put(inverse_low, rows, columns, inverse[rows, columns])
        for rows, columns in tiles:
            part = product(gap_low[rows, :], moment_low[:, columns])
            values = (25.0 * moment[rows, columns] + part) * (1.0 / 16.0)
            mixed[rows, columns] = values
            put(mixed_low, rows, columns, values)
        for rows, columns in tiles:
            part = product(gap_low[rows, :], mixed_low[:, columns])
            values = (25.0 * mixed[rows, columns] + part) * (1.0 / 16.0)
            moment[rows, columns] = values
            put(moment_low, rows, columns, values)
        return level * 1.25 if with_inverse else level

    sweep(False, 0, None)
    level = lax.fori_loop(1, ITERS - 1, functools.partial(sweep, True), jnp.float32(1.25))
    scale = 1.0 / jnp.sqrt(jnp.sqrt(trace_value))
    own_root = roots.at[core]

    def trade_half(rows):
        push(own_root.at[rows], own_root.at[rows], 6, sibling, q).start()

    for rows, columns in tiles:
        root = next_inverse(rows, columns, level)
        if rows.start // half == columns.start // half:
            spots = [
                lax.broadcasted_iota(jnp.int32, (side, half), dim) for dim in range(2)
            ]
            diagonal = spots[1] - spots[0] == rows.start - columns.start
            root += jnp.where(diagonal, 1.25 * level, 0.0)
        put(own_root, rows, columns, root * scale)
        if (rows, columns) == tiles[3]:
            trade_half(left_half)
    trade = push(own_root, own_root, 6, sibling, q)
    trade_half(right_half)

    pl.when(core == 1)(trade.wait_recv)
    quarters = [(rows, columns) for columns in (left_half, right_half) for rows in (left_half, right_half)]
    for rows, columns in quarters:
        hidden = product(roots[0, rows, :], block_all[:, columns])
        gap_low[rows, columns] = hidden.astype(BF16)
    pl.when(core == 0)(trade.wait_recv)
    shaped_total = jnp.zeros((1, 1), F32)
    for rows, columns in quarters:
        shaped = product(gap_low[rows, :], roots[1, :, columns])
        mixed[rows, columns] = shaped
        shaped_total += total(shaped * shaped)
    ratio = jnp.sqrt(grad_total / (shaped_total + graft_eps))
    out_rows[...] = (mixed[...] * ratio).astype(BF16).reshape(out_rows.shape)

    @pl.loop(1, chip_count, unroll=True)
    def _(d):
        t = chip_at(d)
        push(out_rows.at[t, core], update_ref.at[chip], 7, 2 * t + core, q).start()

    keep_here(out_rows.at[chip, core], update_ref.at[chip], 7)

    arrived(routed_in, 5)
    for c in range(CAPS):
        entry = table[0, f * CAPS + c]
        used = entry > 0
        odd = lax.rem(lax.max(entry - 1, 0), 2) == 1
        keep = jnp.where(used, keep_weight, 1.0)
        fresh = jnp.where(used, fresh_weight, 0.0)
        fresh_right = jnp.where(odd, fresh, 0.0)
        source = routed_in[:, c].reshape(width, width)
        gram = (fresh - fresh_right) * rows_gram(source) + fresh_right * columns_gram(source)
        new_ref[c] = keep * old_wide[c] + gram

    arrived(update_ref, 7)

    def all_left(stage, e):
        left_here(spread[stage][e].at[pl.ds(0, chip_count - 1)], FIRST[stage])
        left_here(spread[stage][1 - e], FIRST[stage])
        left_here(chosen[stage][e], 4)

    for stage in range(STAGES):
        for e in range(2):
            pl.when(core == e)(functools.partial(all_left, stage, e))

    far_push.wait_send()
    left_here(grads.at[pl.ds(0, chip_count - 1)], 2)
    left_here(routed.at[pl.ds(0, fsdp_count - 1)], 5)
    trade.wait_send()
    left_here(out_rows.at[pl.ds(0, chip_count - 1), 0], 7)


def write_out(update_ref, stats_ref, update_out, stats_out, sems):
    copies = [pltpu.make_async_copy(update_ref, update_out, sems.at[CAPS])]
    for c in range(CAPS):
        copies.append(pltpu.make_async_copy(stats_ref.at[c], stats_out.at[c], sems.at[c]))
    for copy in copies:
        copy.start()
    for copy in copies:
        copy.wait()


def body(gradients, old_stats, stat_slot):
    fsdp_count = lax.axis_size("fsdp")
    chip_count = fsdp_count // 2
    blk_count, row_count, width = gradients.shape
    stat_count = stat_slot.shape[0]
    side = width // SPLIT
    square = (width, width)
    piece = (row_count, side)
    vmem = pltpu.VMEM

    def staged(*lead):
        def of(stage, e):
            parts = sum(place[:2] == (stage, e) for place in PLACES)
            return vmem((*lead, parts, *piece), BF16)

        return [[of(stage, e) for e in range(2)] for stage in range(STAGES)]

    update, new_stats = pl.pallas_call(
        kernel,
        out_shape=(
            pltpu.VMEM(gradients.shape, gradients.dtype),
            pltpu.VMEM(old_stats.shape, old_stats.dtype),
        ),
        in_specs=[pl.BlockSpec(memory_space=pltpu.HBM)] * 3,
        out_specs=(pl.BlockSpec(memory_space=pl.ANY), pl.BlockSpec(memory_space=pltpu.VMEM)),
        scratch_shapes=[
            pltpu.SMEM((1, stat_count), jnp.int32),
            vmem((1, stat_count), jnp.int32),
            vmem((1, stat_count), jnp.int32),
            pltpu.SMEM((1, stat_count), jnp.int32),
            vmem((CAPS, *square), F32),
            staged(chip_count, CAPS),
            staged(fsdp_count, CAPS),
            staged(fsdp_count),
            vmem((chip_count, len(PLACES), *piece), BF16),
            vmem((blk_count, row_count, width), BF16),
            vmem((blk_count, row_count, width), BF16),
            vmem((chip_count, 2, row_count, width), BF16),
            vmem(square, BF16),
            vmem((fsdp_count, CAPS, row_count, width), BF16),
            vmem((fsdp_count, CAPS, row_count, width), BF16),
            vmem((2, *square), BF16),
            vmem(square, F32),
            vmem(square, BF16),
            vmem(square, BF16),
            vmem(square, F32),
            vmem(square, BF16),
            vmem(square, F32),
            vmem(square, BF16),
            vmem((chip_count, 2, row_count, width), BF16),
            pltpu.SemaphoreType.DMA((CAPS,)),
            pltpu.SemaphoreType.DMA((3,)),
            pltpu.SemaphoreType.REGULAR,
            pltpu.SemaphoreType.DMA((9,)),
            pltpu.SemaphoreType.DMA((9,)),
        ],
        compiler_params=pltpu.CompilerParams(
            collective_id=0, has_side_effects=True, vmem_limit_bytes=57 * 2**20
        ),
        cost_estimate=pl.CostEstimate(
            flops=60 * width**3, bytes_accessed=5 * 2**20, transcendentals=0
        ),
    )(stat_slot.reshape(1, stat_count), gradients, old_stats)
    return pl.pallas_call(
        write_out,
        out_shape=(
            jax.ShapeDtypeStruct(gradients.shape, gradients.dtype),
            jax.ShapeDtypeStruct(old_stats.shape, old_stats.dtype),
        ),
        in_specs=[pl.BlockSpec(memory_space=pltpu.VMEM)] * 2,
        out_specs=(pl.BlockSpec(memory_space=pltpu.HBM), pl.BlockSpec(memory_space=pltpu.HBM)),
        scratch_shapes=[pltpu.SemaphoreType.DMA((1 + CAPS,))],
        compiler_params=pltpu.CompilerParams(vmem_limit_bytes=2**20),
    )(update, new_stats)


def solution(mesh):
    return jax.shard_map(
        body,
        mesh=mesh,
        in_specs=(P("own", "fsdp", None), P(("fsdp", "own"), None, None), P()),
        out_specs=(P("own", "fsdp", None), P(("fsdp", "own"), None, None)),
        check_vma=False,
    )
```
